32 devices in a mesh: grid: 8 (over z, y), states: 4 (over x, core).
Axes of the slice: x: 2, y: 2, z: 4, core: 2. Of those that a mesh axis runs over, the one named last changes fastest.
Arguments:
- states_in: float32 [4, 128, 32, 128], P('states', 'grid'), may hold values from -10 to 10
- potential: float32 [128, 32, 128], P('grid'), may hold values from -2 to 0.5
- projectors: bfloat16 [8, 16, 8, 4096], P('grid', 'states'), may hold values from -0.0625 to 0.0625
- proj_gains: bfloat16 [8, 16, 8], P('grid', 'states'), may hold values from 1 to 6
- atom_owner: int32 [80], P('grid'), may hold values from 0 to 7, as said below
- atom_rows: int32 [80, 32], P('grid'), may hold values from -1 to 4095, as said below
- wrap_rows: int32 [32], replicated, may hold values from 0 to 31, as said below
Outputs:
- filtered: float32 [4, 128, 32, 128], P('states', 'grid')
The draws below stay inside these ranges and needn't reach their ends.
Inputs may be any that keep to these rules, and one draw needn't show every extreme that they name: `atom_owner`: atom a belongs to tile a // 10. At most 2 atoms of one tile share an owner, and one owner takes exactly 2 atoms of every tile. `atom_rows`: A row r is the line of cells at x = r // 32, y = r % 32. Each list holds distinct rows whose x lies in the atom's own tile of 16 planes, followed by -1 entries; each list has 16 rows or more, and the first atom of every tile fills all 32. wrap_rows[y] = (y + t) mod 32 for one t of 1 to 31.
All inputs are finite; a program needn't handle non-finite values.
Results may differ from the reference program's by a relative error of at most 0.00082.
Values may be sent and summed in bfloat16 or wider, within the bound.
A program may use at most 64 MiB of HBM per device.

```python
import math
import jax
import jax.numpy as jnp
from jax import lax

STATES_DEV = 1
CX = 16
NY = 32
NZ = 128
RADIUS = 6
NPROJ = 8
BLK = 32
HOME_ATOMS = 10
PAIR_CAP = 2
NSTATES = 4
NX = 128
OWNERS = 8
ATOMS = 80
SLOTS = 16
N_STATES = 4


def draw_atom_owner(key, part):
    subkeys = jax.random.split(jax.random.fold_in(key, 11), 2)
    busy_owner = jax.random.randint(subkeys[0], (), 0, OWNERS)

    def one_home(home_key):
        key_a, key_b, key_c = jax.random.split(home_key, 3)
        others = jax.random.permutation(key_a, OWNERS - 1)
        others = others + (others >= busy_owner).astype(jnp.int32)
        offset_flip = jax.random.randint(key_b, (), 0, 2)
        slot_order = jnp.arange(HOME_ATOMS, dtype=jnp.int32)
        other_index = jnp.maximum(slot_order - 2 + offset_flip, 0) // 2
        owner_list = jnp.where(slot_order < 2, busy_owner, others[other_index])
        return jax.random.permutation(key_c, owner_list)
    homes = jax.vmap(one_home)(jax.random.split(subkeys[1], OWNERS))
    return homes.reshape(-1).astype(jnp.int32)


def draw_atom_rows(key, part):
    tile_lines = CX * NY
    atom_ids = jnp.arange(ATOMS, dtype=jnp.int32)

    def one_atom(atom_key, atom_id):
        key_a, key_b = jax.random.split(atom_key)
        chosen = jax.random.permutation(key_a, tile_lines)[:BLK]
        live_count = jax.random.randint(key_b, (), BLK // 2, BLK + 1)
        live_count = jnp.where(atom_id % HOME_ATOMS == 0, BLK, live_count)
        row_list = atom_id // HOME_ATOMS * tile_lines + chosen
        return jnp.where(jnp.arange(BLK) < live_count, row_list, -1).astype(jnp.int32)
    return jax.vmap(one_atom)(jax.random.split(jax.random.fold_in(key, 23), ATOMS), atom_ids)


def draw_wrap_rows(key, part):
    skew_shift = jax.random.randint(jax.random.fold_in(key, 37), (), 1, NY)
    return ((jnp.arange(NY, dtype=jnp.int32) + skew_shift) % NY).astype(jnp.int32)


def projector_values(key):
    scale_factor = (BLK * NZ) ** (-0.5)
    full_shape = (OWNERS, SLOTS, NPROJ, BLK * NZ)
    proj_key = jax.random.fold_in(key, 41)
    raw_values = jax.random.truncated_normal(proj_key, -4.0, 4.0, full_shape, jnp.float32)
    return raw_values * scale_factor


def draw_projectors(key, part):
    return projector_values(key).astype(jnp.bfloat16)


def draw_states_in(key, part):
    spread = 0.25 * (BLK * NZ) ** 0.5
    owner_table = draw_atom_owner(key, part).reshape(OWNERS, HOME_ATOMS)
    row_lists = draw_atom_rows(key, part)
    home_order = jnp.arange(HOME_ATOMS, dtype=jnp.int32)
    same_owner = (owner_table[:, :, None] == owner_table[:, None, :]) & (home_order[None, None, :] < home_order[None, :, None])
    owner_rank = jnp.sum(same_owner.astype(jnp.int32), axis=2)
    home_index = jnp.arange(OWNERS, dtype=jnp.int32)[:, None]
    slot_index = (owner_table * SLOTS + home_index * PAIR_CAP + owner_rank).reshape(-1).astype(jnp.int32)
    atom_proj = jnp.take(projector_values(key).reshape(OWNERS * SLOTS, NPROJ, BLK * NZ), slot_index, axis=0)
    safe_rows = jnp.where(row_lists >= 0, row_lists, NX * NY).reshape(-1).astype(jnp.int32)
    noise_key = jax.random.fold_in(key, 53)
    mixing_key = jax.random.fold_in(key, 59)
    line_shape = (NSTATES, NX * NY, NZ)
    mixing_shape = (NSTATES, ATOMS, NPROJ)
    base_lines = jax.random.truncated_normal(noise_key, -4.0, 4.0, line_shape, jnp.float32)
    mixing = jax.random.truncated_normal(mixing_key, -3.0, 3.0, mixing_shape, jnp.float32) * spread

    def one_state(state_pair):
        line_values, state_mixing = state_pair
        aligned = jnp.zeros((ATOMS, BLK * NZ), jnp.float32)
        for proj_index in range(NPROJ):
            aligned = aligned + atom_proj[:, proj_index] * state_mixing[:, proj_index][:, None]
        return line_values.at[safe_rows].add(aligned.reshape(ATOMS * BLK, NZ), mode='drop')
    states = lax.map(one_state, (base_lines, mixing))
    return jnp.clip(states, -10.0, 10.0).reshape(NSTATES, NX, NY, NZ)


def block_levels(rng, shape, cuts, least, high):
    factor_of, own = 1.0, jax.random.fold_in(rng, 6)
    for axis_at, parts in cuts:
        steps = jnp.exp(jax.random.uniform(jax.random.fold_in(own, axis_at), (parts,), jnp.float32, least / len(cuts), high / len(cuts)))
        factor_of = factor_of * jnp.repeat(steps, shape[axis_at] // parts).reshape([-1 if axis == axis_at else 1 for axis in range(len(shape))])
    return factor_of


def setup_inputs(seed: int = 0) -> dict:
    keys = jax.random.split(jax.random.key(seed), 8)
    states_in = draw_states_in(jax.random.fold_in(keys[7], 71), 0)
    potential = jnp.clip(-2.0 + 2.5 * jax.random.uniform(keys[1], (NX, NY, NZ), jnp.float32) ** block_levels(keys[1], (NX, NY, NZ), ((0, 8),), -0.2, 0.2), -2.0, 0.5)
    projectors = draw_projectors(jax.random.fold_in(keys[7], 71), 0)
    proj_gains = jnp.clip(1.0 + 5.0 * jax.random.uniform(keys[3], (OWNERS, SLOTS, NPROJ), jnp.float32) ** block_levels(keys[3], (OWNERS, SLOTS, NPROJ), ((0, 8), (1, 4)), -0.2, 0.2), 1.0, 6.0).astype(jnp.bfloat16)
    atom_owner = draw_atom_owner(jax.random.fold_in(keys[7], 71), 0)
    atom_rows = draw_atom_rows(jax.random.fold_in(keys[7], 71), 0)
    wrap_rows = draw_wrap_rows(jax.random.fold_in(keys[7], 71), 0)
    return dict(states_in=states_in, potential=potential, projectors=projectors, proj_gains=proj_gains, atom_owner=atom_owner, atom_rows=atom_rows, wrap_rows=wrap_rows)


MIXED_WEIGHT = 0.7
CENTER = 12.0
HALF_WIDTH = 8.0


def second_table(radius):
    weights = [-2.0 * sum(1.0 / (k * k) for k in range(1, radius + 1))]
    for k in range(1, radius + 1):
        weights.append(2.0 * (-1) ** (k + 1) * math.factorial(radius) ** 2 / (k * k * math.factorial(radius - k) * math.factorial(radius + k)))
    return weights


def first_table(radius):
    weights = [0.0]
    for k in range(1, radius + 1):
        weights.append((-1) ** (k + 1) * math.factorial(radius) ** 2 / (k * math.factorial(radius - k) * math.factorial(radius + k)))
    return weights


def laplacian(padded, plane_count):
    second_weights = second_table(RADIUS)
    first_weights = first_table(RADIUS)
    interior = padded[:, RADIUS:RADIUS + plane_count]
    line_depth = interior.shape[3]
    z_padded = jnp.pad(interior, ((0, 0), (0, 0), (0, 0), (RADIUS, RADIUS)))
    summed = 3.0 * second_weights[0] * interior
    y_slope = jnp.zeros_like(padded)
    for k in range(1, RADIUS + 1):
        summed = summed + second_weights[k] * (padded[:, RADIUS + k:RADIUS + k + plane_count] + padded[:, RADIUS - k:RADIUS - k + plane_count])
        summed = summed + second_weights[k] * (jnp.roll(interior, -k, 2) + jnp.roll(interior, k, 2))
        summed = summed + second_weights[k] * (z_padded[:, :, :, RADIUS + k:RADIUS + k + line_depth] + z_padded[:, :, :, RADIUS - k:RADIUS - k + line_depth])
        y_slope = y_slope + first_weights[k] * (jnp.roll(padded, -k, 2) - jnp.roll(padded, k, 2))
    cross_term = jnp.zeros_like(interior)
    for k in range(1, RADIUS + 1):
        cross_term = cross_term + first_weights[k] * (y_slope[:, RADIUS + k:RADIUS + k + plane_count] - y_slope[:, RADIUS - k:RADIUS - k + plane_count])
    return summed + MIXED_WEIGHT * cross_term


def extend(grid_field, wrap_rows, unwrap_rows):
    low_rim = jnp.take(grid_field[:, NX - RADIUS:], wrap_rows, axis=2)
    high_rim = jnp.take(grid_field[:, :RADIUS], unwrap_rows, axis=2)
    return jnp.concatenate([low_rim, grid_field, high_rim], axis=1)


def atom_tables(projectors, proj_gains, atom_owner, atom_rows):
    owners = atom_owner.reshape(OWNERS, HOME_ATOMS)
    row_order = jnp.arange(HOME_ATOMS, dtype=jnp.int32)
    same_owner = (owners[:, :, None] == owners[:, None, :]) & (row_order[None, None, :] < row_order[None, :, None])
    owner_rank = jnp.sum(same_owner.astype(jnp.int32), axis=2)
    home_index = jnp.arange(OWNERS, dtype=jnp.int32)[:, None]
    slot_index = (owners * SLOTS + home_index * PAIR_CAP + owner_rank).reshape(-1).astype(jnp.int32)
    atom_proj = jnp.take(projectors.reshape(OWNERS * SLOTS, NPROJ, BLK * NZ), slot_index, axis=0)
    atom_gain = jnp.take(proj_gains.reshape(OWNERS * SLOTS, NPROJ), slot_index, axis=0)
    safe_rows = jnp.where(atom_rows >= 0, atom_rows, NX * NY).astype(jnp.int32)
    return atom_proj, atom_gain, safe_rows


def nonlocal_term(grid_field, atom_proj, atom_gain, safe_rows):
    state_count = grid_field.shape[0]
    tile_lines = grid_field.reshape(state_count, NX * NY, NZ)
    picked = jnp.take(tile_lines, safe_rows, axis=1, mode="fill", fill_value=0.0).astype(jnp.bfloat16)
    picked = picked.reshape(state_count, ATOMS, BLK * NZ)
    coefficients = jnp.einsum("ajc,sac->saj", atom_proj.astype(jnp.float32), picked.astype(jnp.float32))
    scaled = (coefficients * atom_gain.astype(jnp.float32)[None]).astype(jnp.bfloat16)
    projected = jnp.einsum("ajc,saj->sac", atom_proj.astype(jnp.float32), scaled.astype(jnp.float32)).astype(jnp.bfloat16)
    pieces = projected.reshape(state_count, ATOMS, BLK, NZ).astype(jnp.float32)
    summed = jnp.zeros((state_count, NX * NY, NZ), jnp.float32).at[:, safe_rows].add(pieces, mode="drop")
    return summed.reshape(state_count, NX, NY, NZ)


def reference(states_in, potential, projectors, proj_gains, atom_owner, atom_rows, wrap_rows):
    row_order = jnp.arange(NY, dtype=jnp.int32)
    unwrap_rows = jnp.sum(row_order[None, :] * (wrap_rows[None, :] == row_order[:, None]).astype(jnp.int32), axis=1).astype(jnp.int32)
    atom_proj, atom_gain, safe_rows = atom_tables(projectors, proj_gains, atom_owner, atom_rows)

    def operate(grid_field):
        padded = extend(grid_field, wrap_rows, unwrap_rows)
        return -0.5 * laplacian(padded, NX) + potential[None] * grid_field + nonlocal_term(grid_field, atom_proj, atom_gain, safe_rows)

    def shifted(grid_field):
        return (operate(grid_field) - CENTER * grid_field) / HALF_WIDTH

    def filter_group(state_group):
        first_term = shifted(state_group)
        second_term = 2.0 * shifted(first_term) - state_group
        return 2.0 * shifted(second_term) - first_term

    groups = states_in.reshape(N_STATES, STATES_DEV, NX, NY, NZ)
    return lax.map(filter_group, groups).reshape(NSTATES, NX, NY, NZ)
```

```python
import functools
import math

import jax
import jax.numpy as jnp
import ml_dtypes
import numpy as np
from jax import lax
from jax.experimental import pallas as pl
from jax.experimental.pallas import tpu as pltpu
from jax.sharding import PartitionSpec as P

RADIUS = 6
PAIR_CAP = 2
ATOM_PAD = 16

MIXED_WEIGHT = 0.7
CENTER = 12.0
HALF_WIDTH = 8.0

MESH = pl.DeviceIdType.MESH
F32 = jnp.float32
BF16 = jnp.bfloat16


def second_table(radius):
    weights = [-2.0 * sum((1.0 / (k * k) for k in range(1, radius + 1)))]
    for k in range(1, radius + 1):
        weights.append(
            2.0
            * (-1) ** (k + 1)
            * math.factorial(radius) ** 2
            / (k * k * math.factorial(radius - k) * math.factorial(radius + k))
        )
    return weights


def first_table(radius):
    weights = [0.0]
    for k in range(1, radius + 1):
        weights.append(
            (-1) ** (k + 1)
            * math.factorial(radius) ** 2
            / (k * math.factorial(radius - k) * math.factorial(radius + k))
        )
    return weights


def stencil_matrices(planes, breadth, depth):
    second, first = second_table(RADIUS), first_table(RADIUS)
    factor = -0.5 / HALF_WIDTH
    steps = range(1, RADIUS + 1)
    wide = planes + 2 * RADIUS
    lines = np.zeros((planes, breadth, wide, breadth))
    rows = np.arange(breadth)
    for x in range(planes):
        centre = x + RADIUS
        for k in steps:
            for sign in (1, -1):
                lines[x, rows, centre + sign * k, rows] += second[k]
                lines[x, rows, centre, (rows + sign * k) % breadth] += second[k]
                for j in steps:
                    for turn in (1, -1):
                        lines[x, rows, centre + sign * k, (rows + turn * j) % breadth] += (
                            MIXED_WEIGHT * sign * turn * first[k] * first[j]
                        )
    lines = factor * lines.reshape(planes * breadth, wide * breadth)
    across = np.zeros((depth, depth))
    for k in steps:
        across += second[k] * (np.eye(depth, k=k) + np.eye(depth, k=-k))
    rim = RADIUS * breadth
    inner = lines[:, rim:-rim]
    low = lines[:rim, :rim]
    high = lines[-rim:, -rim:]
    return inner, low, high, factor * across, factor * 3.0 * second[0]


def halves(matrix):
    high = matrix.astype(ml_dtypes.bfloat16)
    low = (matrix - high.astype(np.float64)).astype(ml_dtypes.bfloat16)
    return high, low


def dot(a, b):
    return jnp.dot(a, b, preferred_element_type=F32)


def kernel(
    dims,
    v_ref,
    pot_ref,
    proj_ref,
    gain_ref,
    owner_ref,
    rows_ref,
    wrap_ref,
    inner_h_ref,
    inner_l_ref,
    rim_ref,
    across_ref,
    out_ref,
    sendbuf,
    arrived,
    parts,
    hi_ref,
    halo,
    pick_ref,
    place_ref,
    rim_turned,
    base_ref,
    part_send,
    part_recv,
    share_send,
    share_recv,
    halo_send,
    halo_recv,
):
    n_grid, n_states, tiles, chunk, breadth, nproj, atoms, centre_weight = dims
    cells, depth = v_ref.shape
    rim = RADIUS * breadth
    blocks = chunk // depth
    slot_rows = PAIR_CAP * nproj
    me_g, me_s = lax.axis_index("grid"), lax.axis_index("states")
    up, down = lax.rem(me_g + 1, n_grid), lax.rem(me_g + n_grid - 1, n_grid)
    holder = me_g // tiles
    partner = me_s + 1 - 2 * lax.rem(me_s, 2)
    twins = [lax.rem(me_s + 2 * d, n_states) for d in range(1, n_states // 2)]

    barrier = pltpu.get_barrier_semaphore()

    def greet(g, s):
        pl.semaphore_signal(barrier, inc=1, device_id=(g, s), device_id_type=MESH)

    for o in range(n_grid):

        @pl.when((me_g != o) | (holder != me_s))
        def _():
            greet(o, holder)

    greet(up, me_s)
    greet(down, me_s)
    greet(me_g, partner)
    for s in twins:
        greet(me_g, s)

    for i in range(tiles):
        held = pl.ds(i * slot_rows, slot_rows)
        for s in range(n_states):
            sendbuf[i, s, :, :chunk] = proj_ref[held, s * chunk : (s + 1) * chunk]
            sendbuf[i, s, :, chunk:] = gain_ref[held, :]
    hi_ref[0] = v_ref[...].astype(BF16)

    pl.semaphore_wait(barrier, n_grid + 2 + len(twins) + jnp.where(holder == me_s, 0, 1))

    def part_copy(i, d):
        s = lax.rem(me_s + d, n_states)
        return pltpu.make_async_remote_copy(
            src_ref=sendbuf.at[i, s],
            dst_ref=arrived.at[me_g],
            send_sem=part_send.at[i, d],
            recv_sem=part_recv.at[me_g],
            device_id=(me_s * tiles + i, s),
            device_id_type=MESH,
        )

    def halo_copies(step):
        return [
            pltpu.make_async_remote_copy(
                src_ref=hi_ref.at[step, pl.ds(start, rim)],
                dst_ref=halo.at[step, side],
                send_sem=halo_send.at[step, side],
                recv_sem=halo_recv.at[step, side],
                device_id=(target, me_s),
                device_id_type=MESH,
            )
            for side, start, target in ((0, cells - rim, up), (1, 0, down))
        ]

    def share_copy(index, part, target):
        return pltpu.make_async_remote_copy(
            src_ref=parts.at[part],
            dst_ref=parts.at[part],
            send_sem=share_send.at[index],
            recv_sem=share_recv.at[part],
            device_id=(me_g, target),
            device_id_type=MESH,
        )

    for d in range(n_states - 1, -1, -1):
        for i in range(tiles):
            if d:
                part_copy(i, d).start()
            else:

                @pl.when(me_s * tiles + i != me_g)
                def _():
                    part_copy(i, 0).start()

                @pl.when(me_s * tiles + i == me_g)
                def _():
                    arrived[me_g] = sendbuf[i, me_s]

    for copy in halo_copies(0):
        copy.start()

    owners = [owner_ref[a] for a in range(atoms)]
    slots = []
    for a in range(atoms):
        rank = jnp.int32(0)
        for b in range(a):
            rank = rank + jnp.where(owners[b] == owners[a], 1, 0)
        slots.append(owners[a] * PAIR_CAP + rank)
    width = n_grid * slot_rows
    lane = lax.broadcasted_iota(jnp.int32, (nproj, width), 1)
    row = lax.broadcasted_iota(jnp.int32, (nproj, width), 0)
    chosen = jnp.concatenate(
        [jnp.where(lane == slots[a] * nproj + row, 1.0, 0.0) for a in range(atoms)], axis=0
    ).astype(BF16)

    block_rows = rows_ref.shape[1]
    local = rows_ref[...] - me_g * cells
    local = jnp.concatenate(
        [local, jnp.full((ATOM_PAD - atoms, block_rows), -1, jnp.int32)], axis=0
    )
    line = lax.broadcasted_iota(jnp.int32, (ATOM_PAD, cells), 1)
    pick = jnp.concatenate(
        [jnp.where(local[:, b : b + 1] == line, 1.0, 0.0) for b in range(block_rows)], axis=0
    )
    pick_ref[...] = pick.astype(BF16)
    place_ref[...] = pick.T.astype(BF16)

    turn = wrap_ref[0]
    source = lax.broadcasted_iota(jnp.int32, (rim, rim), 0)
    target = lax.broadcasted_iota(jnp.int32, (rim, rim), 1)
    low_turn = jnp.where(me_g == 0, turn, 0)
    high_turn = jnp.where(me_g == n_grid - 1, breadth - turn, 0)
    for side, shift in ((0, low_turn), (1, high_turn)):
        same_plane = (source // breadth) == (target // breadth)
        moved = lax.rem(lax.rem(source, breadth) + shift, breadth) == lax.rem(target, breadth)
        permute = jnp.where(same_plane & moved, 1.0, 0.0).astype(BF16)
        for half in range(2):
            rim_turned[side, half] = dot(rim_ref[side, half], permute).astype(BF16)

    base_ref[...] = (pot_ref[...] - CENTER) * (1.0 / HALF_WIDTH) + centre_weight

    def own_cells(step, field):
        hi = hi_ref[step]
        lo = (field - hi.astype(F32)).astype(BF16)
        both = jnp.concatenate([hi, lo], axis=1)
        wide = dot(inner_h_ref[...], both)
        total = base_ref[...] * field
        total = total + (wide[:, :depth] + wide[:, depth:] + dot(inner_l_ref[...], hi))
        across = dot(hi, across_ref[...])
        total = total + (across[:, :depth] + across[:, depth:])
        return total + dot(lo, across_ref[:, :depth])

    def rims(step):
        for copy in halo_copies(step):
            copy.wait_recv()
        sums = []
        for side in range(2):
            came = halo[step, side]
            sums.append(dot(rim_turned[side, 0], came) + dot(rim_turned[side, 1], came))
        middle = jnp.zeros((cells - 2 * rim, depth), F32)
        return jnp.concatenate([sums[0], middle, sums[1]], axis=0)

    def nonlocal_part(step, gains):
        picked = dot(pick_ref[...], hi_ref[step]).astype(BF16)
        coefficients = jnp.zeros((ATOM_PAD, atoms * nproj), F32)
        for q in range(n_states):
            lines = [
                picked[(q * blocks + b) * ATOM_PAD : (q * blocks + b + 1) * ATOM_PAD]
                for b in range(blocks)
            ]
            coefficients = coefficients + lax.dot_general(
                jnp.concatenate(lines, axis=1),
                parts[q],
                (((1,), (1,)), ((), ())),
                preferred_element_type=F32,
            )
        atom = lax.broadcasted_iota(jnp.int32, coefficients.shape, 0)
        column = lax.broadcasted_iota(jnp.int32, coefficients.shape, 1)
        scaled = jnp.where(column // nproj == atom, coefficients * gains, 0.0).astype(BF16)
        pieces = []
        for q in range(n_states):
            projected = dot(scaled, parts[q]).astype(BF16)
            pieces += [projected[:, b * depth : (b + 1) * depth] for b in range(blocks)]
        return dot(place_ref[...], jnp.concatenate(pieces, axis=0)) * (1.0 / HALF_WIDTH)

    start = v_ref[...]
    first = own_cells(0, start)
    first = first + rims(0)

    for o in range(n_grid):

        @pl.when((me_g != o) | (holder != me_s))
        def _():
            pltpu.make_async_remote_copy(
                src_ref=sendbuf.at[0, 0],
                dst_ref=arrived.at[o],
                send_sem=part_send.at[0, 0],
                recv_sem=part_recv.at[o],
                device_id=(o, holder),
                device_id_type=MESH,
            ).wait_recv()

    mine = dot(chosen, arrived[...].reshape(width, chunk + depth))
    parts[me_s] = mine[:, :chunk].astype(BF16)
    for index, s in enumerate(twins):
        share_copy(1 + index, me_s, s).start()
    share_copy(0, me_s, partner).start()
    gains = mine[:, chunk:].T[0:1]
    for index, s in enumerate(twins):
        share_copy(0, s, partner).wait_recv()
        share_copy(1 + len(twins) + index, s, partner).start()
    share_copy(0, partner, partner).wait_recv()
    for s in twins:
        share_copy(0, s + 1 - 2 * lax.rem(s, 2), partner).wait_recv()

    first = first + nonlocal_part(0, gains)
    hi_ref[1] = first.astype(BF16)
    for copy in halo_copies(1):
        copy.start()
    second = own_cells(1, first) + nonlocal_part(1, gains)
    second = 2.0 * (second + rims(1)) - start
    hi_ref[2] = second.astype(BF16)
    for copy in halo_copies(2):
        copy.start()
    last = own_cells(2, second) + nonlocal_part(2, gains)
    out_ref[...] = 2.0 * (last + rims(2)) - first

    for d in range(n_states):
        for i in range(tiles):
            if d:
                part_copy(i, d).wait_send()
            else:

                @pl.when(me_s * tiles + i != me_g)
                def _():
                    part_copy(i, 0).wait_send()

    share_copy(0, me_s, partner).wait_send()
    for index, s in enumerate(twins):
        share_copy(1 + index, me_s, s).wait_send()
        share_copy(1 + len(twins) + index, s, partner).wait_send()
    for step in range(3):
        for copy in halo_copies(step):
            copy.wait_send()


def shards(states_in, potential, projectors, proj_gains, atom_owner, atom_rows, wrap_rows):
    _, planes, breadth, depth = states_in.shape
    n_grid, n_states = lax.axis_size("grid"), lax.axis_size("states")
    _, held, nproj, span = projectors.shape
    atoms = atom_owner.shape[0]
    cells, rim = planes * breadth, RADIUS * breadth
    tiles = held // PAIR_CAP
    chunk = span // n_states
    slot_rows = PAIR_CAP * nproj
    inner, low, high, across, centre_weight = stencil_matrices(planes, breadth, depth)
    inner_h, inner_l = halves(inner)
    rim_matrices = np.stack([np.stack(halves(low)), np.stack(halves(high))])
    across_both = np.concatenate(halves(across), axis=1)
    gains = jnp.broadcast_to(proj_gains.reshape(held * nproj, 1), (held * nproj, depth))
    dims = (n_grid, n_states, tiles, chunk, breadth, nproj, atoms, centre_weight)
    vmem = pl.BlockSpec(memory_space=pltpu.VMEM)
    smem = pl.BlockSpec(memory_space=pltpu.SMEM)
    flops = 2 * 3 * depth * cells * (5 * cells + 3 * depth)
    out = pl.pallas_call(
        functools.partial(kernel, dims),
        out_shape=jax.ShapeDtypeStruct((cells, depth), F32),
        in_specs=[vmem, vmem, vmem, vmem, smem, vmem, smem, vmem, vmem, vmem, vmem],
        out_specs=vmem,
        scratch_shapes=[
            pltpu.VMEM((tiles, n_states, slot_rows, chunk + depth), BF16),
            pltpu.VMEM((n_grid, slot_rows, chunk + depth), BF16),
            pltpu.VMEM((n_states, atoms * nproj, chunk), BF16),
            pltpu.VMEM((3, cells, depth), BF16),
            pltpu.VMEM((3, 2, rim, depth), BF16),
            pltpu.VMEM((ATOM_PAD * atom_rows.shape[1], cells), BF16),
            pltpu.VMEM((cells, ATOM_PAD * atom_rows.shape[1]), BF16),
            pltpu.VMEM((2, 2, rim, rim), BF16),
            pltpu.VMEM((cells, depth), F32),
            pltpu.SemaphoreType.DMA((tiles, n_states)),
            pltpu.SemaphoreType.DMA((n_grid,)),
            pltpu.SemaphoreType.DMA((n_states,)),
            pltpu.SemaphoreType.DMA((n_states,)),
            pltpu.SemaphoreType.DMA((3, 2)),
            pltpu.SemaphoreType.DMA((3, 2)),
        ],
        compiler_params=pltpu.CompilerParams(
            collective_id=0, has_side_effects=True, vmem_limit_bytes=40 * 1024 * 1024
        ),
        cost_estimate=pl.CostEstimate(
            flops=flops, bytes_accessed=4 * 1024 * 1024, transcendentals=0
        ),
    )(
        states_in.reshape(cells, depth),
        potential.reshape(cells, depth),
        projectors.reshape(held * nproj, span),
        gains,
        atom_owner,
        atom_rows,
        wrap_rows,
        jnp.asarray(inner_h),
        jnp.asarray(inner_l),
        jnp.asarray(rim_matrices),
        jnp.asarray(across_both),
    )
    return out.reshape(states_in.shape)


def solution(mesh):
    in_specs = (
        P("states", "grid", None, None),
        P("grid", None, None),
        P("grid", "states", None, None),
        P("grid", "states", None),
        P("grid"),
        P("grid", None),
        P(),
    )
    out_specs = P("states", "grid", None, None)
    return jax.shard_map(shards, mesh=mesh, in_specs=in_specs, out_specs=out_specs, check_vma=False)
```

```python
import functools
import math

import jax
import jax.numpy as jnp
import ml_dtypes
import numpy as np
from jax import lax
from jax.experimental import pallas as pl
from jax.experimental.pallas import tpu as pltpu
from jax.sharding import PartitionSpec as P

RADIUS = 6
PAIR_CAP = 2
ATOM_PAD = 16
PIECES = 2

MIXED_WEIGHT = 0.7
CENTER = 12.0
HALF_WIDTH = 8.0

MESH = pl.DeviceIdType.MESH
F32 = jnp.float32
BF16 = jnp.bfloat16


def second_table(radius):
    weights = [-2.0 * sum((1.0 / (k * k) for k in range(1, radius + 1)))]
    for k in range(1, radius + 1):
        weights.append(
            2.0
            * (-1) ** (k + 1)
            * math.factorial(radius) ** 2
            / (k * k * math.factorial(radius - k) * math.factorial(radius + k))
        )
    return weights


def first_table(radius):
    weights = [0.0]
    for k in range(1, radius + 1):
        weights.append(
            (-1) ** (k + 1)
            * math.factorial(radius) ** 2
            / (k * math.factorial(radius - k) * math.factorial(radius + k))
        )
    return weights


def stencil_matrices(planes, breadth, depth):
    second, first = second_table(RADIUS), first_table(RADIUS)
    factor = -0.5 / HALF_WIDTH
    steps = range(1, RADIUS + 1)
    wide = planes + 2 * RADIUS
    lines = np.zeros((planes, breadth, wide, breadth))
    rows = np.arange(breadth)
    for x in range(planes):
        centre = x + RADIUS
        for k in steps:
            for sign in (1, -1):
                lines[x, rows, centre + sign * k, rows] += second[k]
                lines[x, rows, centre, (rows + sign * k) % breadth] += second[k]
                for j in steps:
                    for turn in (1, -1):
                        lines[x, rows, centre + sign * k, (rows + turn * j) % breadth] += (
                            MIXED_WEIGHT * sign * turn * first[k] * first[j]
                        )
    lines = factor * lines.reshape(planes * breadth, wide * breadth)
    across = np.zeros((depth, depth))
    for k in steps:
        across += second[k] * (np.eye(depth, k=k) + np.eye(depth, k=-k))
    rim = RADIUS * breadth
    inner = lines[:, rim:-rim]
    low = lines[:rim, :rim]
    high = lines[-rim:, -rim:]
    return inner, low, high, factor * across, factor * 3.0 * second[0]


def halves(matrix):
    high = matrix.astype(ml_dtypes.bfloat16)
    low = (matrix - high.astype(np.float64)).astype(ml_dtypes.bfloat16)
    return high, low


def dot(a, b):
    return jnp.dot(a, b, preferred_element_type=F32)


def kernel(
    dims,
    v_hbm,
    pot_hbm,
    proj_hbm,
    inner_h_hbm,
    inner_l_hbm,
    rim_hbm,
    across_hbm,
    gain_ref,
    owner_ref,
    rows_ref,
    wrap_ref,
    out_ref,
    v_ref,
    pot_ref,
    inner_h_ref,
    inner_l_ref,
    rim_ref,
    across_ref,
    sendbuf,
    sendbuf_last,
    arrived,
    arrived_last,
    parts,
    hi_ref,
    halo,
    pick_ref,
    place_ref,
    rim_turned,
    base_ref,
    load_sem,
    piece_sem,
    part_send,
    part_recv,
    share_send,
    share_recv,
    halo_send,
    halo_recv,
):
    n_grid, n_states, tiles, chunk, breadth, nproj, atoms, centre_weight = dims
    cells, depth = v_ref.shape
    rim = RADIUS * breadth
    piece = chunk // PIECES
    blocks = piece // depth
    slot_rows = PAIR_CAP * nproj
    me_g, me_s = lax.axis_index("grid"), lax.axis_index("states")
    up, down = lax.rem(me_g + 1, n_grid), lax.rem(me_g + n_grid - 1, n_grid)
    holder = me_g // tiles
    partner = me_s + 1 - 2 * lax.rem(me_s, 2)
    twins = [lax.rem(me_s + 2 * d, n_states) for d in range(1, n_states // 2)]

    def outgoing(h, i, s):
        return sendbuf_last.at[i, s] if h == PIECES - 1 else sendbuf.at[h, i, s]

    def incoming(h, o):
        return arrived_last.at[o] if h == PIECES - 1 else arrived.at[h, o]

    piece_loads = [
        pltpu.make_async_copy(
            proj_hbm.at[pl.ds(i * slot_rows, slot_rows), pl.ds(s * chunk + h * piece, piece)],
            outgoing(h, i, s).at[:, pl.ds(0, piece)],
            piece_sem.at[h, i, s],
        )
        for h in range(PIECES)
        for i in range(tiles)
        for s in range(n_states)
    ]
    load_v, load_pot, *load_tables = [
        pltpu.make_async_copy(src, dst, load_sem.at[n])
        for n, (src, dst) in enumerate(
            (
                (v_hbm, v_ref),
                (pot_hbm, pot_ref),
                (inner_h_hbm, inner_h_ref),
                (inner_l_hbm, inner_l_ref),
                (rim_hbm, rim_ref),
                (across_hbm, across_ref),
            )
        )
    ]
    load_v.start()
    for load in piece_loads:
        load.start()
    load_pot.start()
    for load in load_tables:
        load.start()

    barrier = pltpu.get_barrier_semaphore()

    def greet(g, s):
        pl.semaphore_signal(barrier, inc=1, device_id=(g, s), device_id_type=MESH)

    for o in range(n_grid):

        @pl.when((me_g != o) | (holder != me_s))
        def _():
            greet(o, holder)

    greet(up, me_s)
    greet(down, me_s)
    greet(me_g, partner)
    for s in twins:
        greet(me_g, s)

    gain_rows = gain_ref[...]
    nothing = jnp.zeros((slot_rows, depth - nproj), BF16)
    below = jnp.zeros((slot_rows - PAIR_CAP, nproj), BF16)
    for i in range(tiles):
        own_rows = gain_rows[i * PAIR_CAP : (i + 1) * PAIR_CAP]
        block = jnp.concatenate([jnp.concatenate([own_rows, below], axis=0), nothing], axis=1)
        for s in range(n_states):
            sendbuf_last[i, s, :, piece:] = block
    load_v.wait()
    hi_ref[0] = v_ref[...].astype(BF16)
    for load in piece_loads:
        load.wait()

    pl.semaphore_wait(barrier, n_grid + 2 + len(twins) + jnp.where(holder == me_s, 0, 1))

    def part_copy(h, i, d):
        s = lax.rem(me_s + d, n_states)
        return pltpu.make_async_remote_copy(
            src_ref=outgoing(h, i, s),
            dst_ref=incoming(h, me_g),
            send_sem=part_send.at[h, i, d],
            recv_sem=part_recv.at[h, me_g],
            device_id=(me_s * tiles + i, s),
            device_id_type=MESH,
        )

    def halo_copies(step):
        return [
            pltpu.make_async_remote_copy(
                src_ref=hi_ref.at[step, pl.ds(start, rim)],
                dst_ref=halo.at[step, side],
                send_sem=halo_send.at[step, side],
                recv_sem=halo_recv.at[step, side],
                device_id=(target, me_s),
                device_id_type=MESH,
            )
            for side, start, target in ((0, cells - rim, up), (1, 0, down))
        ]

    def share_copy(h, index, part, target):
        return pltpu.make_async_remote_copy(
            src_ref=parts.at[part, h],
            dst_ref=parts.at[part, h],
            send_sem=share_send.at[h, index],
            recv_sem=share_recv.at[h, part],
            device_id=(me_g, target),
            device_id_type=MESH,
        )

    for h in range(PIECES):
        for d in range(n_states - 1, -1, -1):
            for i in range(tiles):
                if d:
                    part_copy(h, i, d).start()
                else:

                    @pl.when(me_s * tiles + i != me_g)
                    def _():
                        part_copy(h, i, 0).start()

                    @pl.when(me_s * tiles + i == me_g)
                    def _():
                        incoming(h, me_g)[...] = outgoing(h, i, me_s)[...]

    for copy in halo_copies(0):
        copy.start()

    owners = [owner_ref[a] for a in range(atoms)]
    slots = []
    for a in range(atoms):
        rank = jnp.int32(0)
        for b in range(a):
            rank = rank + jnp.where(owners[b] == owners[a], 1, 0)
        slots.append(owners[a] * PAIR_CAP + rank)
    width = n_grid * slot_rows
    lane = lax.broadcasted_iota(jnp.int32, (nproj, width), 1)
    row = lax.broadcasted_iota(jnp.int32, (nproj, width), 0)
    chosen = jnp.concatenate(
        [jnp.where(lane == slots[a] * nproj + row, 1.0, 0.0) for a in range(atoms)], axis=0
    ).astype(BF16)

    lane = lax.broadcasted_iota(jnp.int32, (1, width), 1)
    places = [(slot // PAIR_CAP) * slot_rows + lax.rem(slot, PAIR_CAP) for slot in slots]
    slot_lines = [jnp.where(lane == place, 1.0, 0.0) for place in places]
    slot_lines = jnp.concatenate(
        slot_lines + [jnp.zeros((ATOM_PAD - atoms, width), F32)], axis=0
    ).astype(BF16)
    spread = jnp.where(
        lax.rem(lax.broadcasted_iota(jnp.int32, (depth, atoms * nproj), 1), nproj)
        == lax.broadcasted_iota(jnp.int32, (depth, atoms * nproj), 0),
        1.0,
        0.0,
    ).astype(BF16)

    block_rows = rows_ref.shape[1]
    local = rows_ref[...] - me_g * cells
    local = jnp.concatenate(
        [local, jnp.full((ATOM_PAD - atoms, block_rows), -1, jnp.int32)], axis=0
    )
    line = lax.broadcasted_iota(jnp.int32, (ATOM_PAD, cells), 1)
    pick = jnp.concatenate(
        [jnp.where(local[:, b : b + 1] == line, 1.0, 0.0) for b in range(block_rows)], axis=0
    )
    pick_ref[...] = pick.astype(BF16)
    place_ref[...] = pick.T.astype(BF16)

    load_pot.wait()
    for load in load_tables:
        load.wait()

    turn = wrap_ref[0]
    source = lax.broadcasted_iota(jnp.int32, (rim, rim), 0)
    target = lax.broadcasted_iota(jnp.int32, (rim, rim), 1)
    low_turn = jnp.where(me_g == 0, turn, 0)
    high_turn = jnp.where(me_g == n_grid - 1, breadth - turn, 0)
    for side, shift in ((0, low_turn), (1, high_turn)):
        same_plane = (source // breadth) == (target // breadth)
        moved = lax.rem(lax.rem(source, breadth) + shift, breadth) == lax.rem(target, breadth)
        permute = jnp.where(same_plane & moved, 1.0, 0.0).astype(BF16)
        for half in range(2):
            rim_turned[side, half] = dot(rim_ref[side, half], permute).astype(BF16)

    base_ref[...] = (pot_ref[...] - CENTER) * (1.0 / HALF_WIDTH) + centre_weight

    def own_cells(step, field):
        hi = hi_ref[step]
        lo = (field - hi.astype(F32)).astype(BF16)
        both = jnp.concatenate([hi, lo], axis=1)
        wide = dot(inner_h_ref[...], both)
        total = base_ref[...] * field
        total = total + (wide[:, :depth] + wide[:, depth:] + dot(inner_l_ref[...], hi))
        across = dot(hi, across_ref[...])
        total = total + (across[:, :depth] + across[:, depth:])
        return total + dot(lo, across_ref[:, :depth])

    def rims(step):
        for copy in halo_copies(step):
            copy.wait_recv()
        sums = []
        for side in range(2):
            came = halo[step, side]
            sums.append(dot(rim_turned[side, 0], came) + dot(rim_turned[side, 1], came))
        middle = jnp.zeros((cells - 2 * rim, depth), F32)
        return jnp.concatenate([sums[0], middle, sums[1]], axis=0)

    def nonlocal_part(step, gains):
        picked = dot(pick_ref[...], hi_ref[step]).astype(BF16)
        coefficients = jnp.zeros((ATOM_PAD, atoms * nproj), F32)
        pairs = [(q, h) for q in range(n_states) for h in range(PIECES)]
        for n, (q, h) in enumerate(pairs):
            lines = [
                picked[b * ATOM_PAD : (b + 1) * ATOM_PAD]
                for b in range(n * blocks, (n + 1) * blocks)
            ]
            coefficients = coefficients + lax.dot_general(
                jnp.concatenate(lines, axis=1),
                parts[q, h],
                (((1,), (1,)), ((), ())),
                preferred_element_type=F32,
            )
        atom = lax.broadcasted_iota(jnp.int32, coefficients.shape, 0)
        column = lax.broadcasted_iota(jnp.int32, coefficients.shape, 1)
        scaled = jnp.where(column // nproj == atom, coefficients * gains, 0.0).astype(BF16)
        pieces = []
        for q, h in pairs:
            projected = dot(scaled, parts[q, h]).astype(BF16)
            pieces += [projected[:, b * depth : (b + 1) * depth] for b in range(blocks)]
        return dot(place_ref[...], jnp.concatenate(pieces, axis=0)) * (1.0 / HALF_WIDTH)

    start = v_ref[...]
    first = own_cells(0, start)
    first = first + rims(0)

    def forward(h):
        for index, s in enumerate(twins):
            share_copy(h, 0, s, partner).wait_recv()
            share_copy(h, 1 + len(twins) + index, s, partner).start()

    for h in range(PIECES):
        for o in range(n_grid):

            @pl.when((me_g != o) | (holder != me_s))
            def _():
                pltpu.make_async_remote_copy(
                    src_ref=outgoing(h, 0, 0),
                    dst_ref=incoming(h, o),
                    send_sem=part_send.at[h, 0, 0],
                    recv_sem=part_recv.at[h, o],
                    device_id=(o, holder),
                    device_id_type=MESH,
                ).wait_recv()

        if h == PIECES - 1:
            came = arrived_last[...].reshape(width, piece + depth)
            parts[me_s, h] = dot(chosen, came[:, :piece]).astype(BF16)
        else:
            parts[me_s, h] = dot(chosen, arrived[h].reshape(width, piece)).astype(BF16)
        for index, s in enumerate(twins):
            share_copy(h, 1 + index, me_s, s).start()
        share_copy(h, 0, me_s, partner).start()
        if h:
            forward(h - 1)
    gains = dot(dot(slot_lines, came[:, piece:]).astype(BF16), spread)
    forward(PIECES - 1)
    for h in range(PIECES):
        share_copy(h, 0, partner, partner).wait_recv()
        for s in twins:
            share_copy(h, 0, s + 1 - 2 * lax.rem(s, 2), partner).wait_recv()

    first = first + nonlocal_part(0, gains)
    hi_ref[1] = first.astype(BF16)
    for copy in halo_copies(1):
        copy.start()
    second = own_cells(1, first) + nonlocal_part(1, gains)
    second = 2.0 * (second + rims(1)) - start
    hi_ref[2] = second.astype(BF16)
    for copy in halo_copies(2):
        copy.start()
    last = own_cells(2, second) + nonlocal_part(2, gains)
    out_ref[...] = 2.0 * (last + rims(2)) - first

    for h in range(PIECES):
        for d in range(n_states):
            for i in range(tiles):
                if d:
                    part_copy(h, i, d).wait_send()
                else:

                    @pl.when(me_s * tiles + i != me_g)
                    def _():
                        part_copy(h, i, 0).wait_send()

        share_copy(h, 0, me_s, partner).wait_send()
        for index, s in enumerate(twins):
            share_copy(h, 1 + index, me_s, s).wait_send()
            share_copy(h, 1 + len(twins) + index, s, partner).wait_send()
    for step in range(3):
        for copy in halo_copies(step):
            copy.wait_send()


def shards(states_in, potential, projectors, proj_gains, atom_owner, atom_rows, wrap_rows):
    _, planes, breadth, depth = states_in.shape
    n_grid, n_states = lax.axis_size("grid"), lax.axis_size("states")
    _, held, nproj, span = projectors.shape
    atoms = atom_owner.shape[0]
    cells, rim = planes * breadth, RADIUS * breadth
    tiles = held // PAIR_CAP
    chunk = span // n_states
    piece = chunk // PIECES
    slot_rows = PAIR_CAP * nproj
    inner, low, high, across, centre_weight = stencil_matrices(planes, breadth, depth)
    inner_h, inner_l = halves(inner)
    rim_matrices = np.stack([np.stack(halves(low)), np.stack(halves(high))])
    across_both = np.concatenate(halves(across), axis=1)
    dims = (n_grid, n_states, tiles, chunk, breadth, nproj, atoms, centre_weight)
    hbm = pl.BlockSpec(memory_space=pltpu.HBM)
    vmem = pl.BlockSpec(memory_space=pltpu.VMEM)
    smem = pl.BlockSpec(memory_space=pltpu.SMEM)
    flops = 2 * 3 * depth * cells * (5 * cells + 3 * depth)
    out = pl.pallas_call(
        functools.partial(kernel, dims),
        out_shape=jax.ShapeDtypeStruct((cells, depth), F32),
        in_specs=[hbm] * 7 + [vmem, smem, vmem, smem],
        out_specs=vmem,
        scratch_shapes=[
            pltpu.VMEM((cells, depth), F32),
            pltpu.VMEM((cells, depth), F32),
            pltpu.VMEM((cells, cells), BF16),
            pltpu.VMEM((cells, cells), BF16),
            pltpu.VMEM((2, 2, rim, rim), BF16),
            pltpu.VMEM((depth, 2 * depth), BF16),
            pltpu.VMEM((PIECES - 1, tiles, n_states, slot_rows, piece), BF16),
            pltpu.VMEM((tiles, n_states, slot_rows, piece + depth), BF16),
            pltpu.VMEM((PIECES - 1, n_grid, slot_rows, piece), BF16),
            pltpu.VMEM((n_grid, slot_rows, piece + depth), BF16),
            pltpu.VMEM((n_states, PIECES, atoms * nproj, piece), BF16),
            pltpu.VMEM((3, cells, depth), BF16),
            pltpu.VMEM((3, 2, rim, depth), BF16),
            pltpu.VMEM((ATOM_PAD * atom_rows.shape[1], cells), BF16),
            pltpu.VMEM((cells, ATOM_PAD * atom_rows.shape[1]), BF16),
            pltpu.VMEM((2, 2, rim, rim), BF16),
            pltpu.VMEM((cells, depth), F32),
            pltpu.SemaphoreType.DMA((6,)),
            pltpu.SemaphoreType.DMA((PIECES, tiles, n_states)),
            pltpu.SemaphoreType.DMA((PIECES, tiles, n_states)),
            pltpu.SemaphoreType.DMA((PIECES, n_grid)),
            pltpu.SemaphoreType.DMA((PIECES, n_states)),
            pltpu.SemaphoreType.DMA((PIECES, n_states)),
            pltpu.SemaphoreType.DMA((3, 2)),
            pltpu.SemaphoreType.DMA((3, 2)),
        ],
        compiler_params=pltpu.CompilerParams(
            collective_id=0, has_side_effects=True, vmem_limit_bytes=63 * 1024 * 1024
        ),
        cost_estimate=pl.CostEstimate(
            flops=flops, bytes_accessed=4 * 1024 * 1024, transcendentals=0
        ),
    )(
        states_in.reshape(cells, depth),
        potential.reshape(cells, depth),
        projectors.reshape(held * nproj, span),
        jnp.asarray(inner_h),
        jnp.asarray(inner_l),
        jnp.asarray(rim_matrices),
        jnp.asarray(across_both),
        proj_gains.reshape(held, nproj),
        atom_owner,
        atom_rows,
        wrap_rows,
    )
    return out.reshape(states_in.shape)


def solution(mesh):
    in_specs = (
        P("states", "grid", None, None),
        P("grid", None, None),
        P("grid", "states", None, None),
        P("grid", "states", None),
        P("grid"),
        P("grid", None),
        P(),
    )
    out_specs = P("states", "grid", None, None)
    return jax.shard_map(shards, mesh=mesh, in_specs=in_specs, out_specs=out_specs, check_vma=False)
```

```python
import functools
import math

import jax
import jax.numpy as jnp
import ml_dtypes
import numpy as np
from jax import lax
from jax.experimental import pallas as pl
from jax.experimental.pallas import tpu as pltpu
from jax.sharding import PartitionSpec as P

RADIUS = 6
PAIR_CAP = 2
ATOM_PAD = 16
PIECES = 2

MIXED_WEIGHT = 0.7
CENTER = 12.0
HALF_WIDTH = 8.0

MESH = pl.DeviceIdType.MESH
F32 = jnp.float32
BF16 = jnp.bfloat16


def second_table(radius):
    weights = [-2.0 * sum((1.0 / (k * k) for k in range(1, radius + 1)))]
    for k in range(1, radius + 1):
        weights.append(
            2.0
            * (-1) ** (k + 1)
            * math.factorial(radius) ** 2
            / (k * k * math.factorial(radius - k) * math.factorial(radius + k))
        )
    return weights


def first_table(radius):
    weights = [0.0]
    for k in range(1, radius + 1):
        weights.append(
            (-1) ** (k + 1)
            * math.factorial(radius) ** 2
            / (k * math.factorial(radius - k) * math.factorial(radius + k))
        )
    return weights


def stencil_matrices(planes, breadth, depth):
    second, first = second_table(RADIUS), first_table(RADIUS)
    factor = -0.5 / HALF_WIDTH
    steps = range(1, RADIUS + 1)
    wide = planes + 2 * RADIUS
    lines = np.zeros((planes, breadth, wide, breadth))
    rows = np.arange(breadth)
    for x in range(planes):
        centre = x + RADIUS
        for k in steps:
            for sign in (1, -1):
                lines[x, rows, centre + sign * k, rows] += second[k]
                lines[x, rows, centre, (rows + sign * k) % breadth] += second[k]
                for j in steps:
                    for turn in (1, -1):
                        lines[x, rows, centre + sign * k, (rows + turn * j) % breadth] += (
                            MIXED_WEIGHT * sign * turn * first[k] * first[j]
                        )
    lines = factor * lines.reshape(planes * breadth, wide * breadth)
    across = np.zeros((depth, depth))
    for k in steps:
        across += second[k] * (np.eye(depth, k=k) + np.eye(depth, k=-k))
    rim = RADIUS * breadth
    inner = lines[:, rim:-rim]
    low = lines[:rim, :rim]
    high = lines[-rim:, -rim:]
    return inner, low, high, factor * across, factor * 3.0 * second[0]


def halves(matrix):
    high = matrix.astype(ml_dtypes.bfloat16)
    low = (matrix - high.astype(np.float64)).astype(ml_dtypes.bfloat16)
    return high, low


def dot(a, b):
    return jnp.dot(a, b, preferred_element_type=F32)


def kernel(
    dims,
    v_hbm,
    pot_hbm,
    proj_hbm,
    inner_h_hbm,
    inner_l_hbm,
    rim_hbm,
    across_hbm,
    gain_ref,
    owner_ref,
    rows_ref,
    wrap_ref,
    out_ref,
    v_ref,
    pot_ref,
    inner_h_ref,
    inner_l_ref,
    rim_ref,
    across_ref,
    sendbuf,
    sendbuf_last,
    arrived,
    arrived_last,
    parts,
    hi_ref,
    halo,
    pick_ref,
    place_ref,
    rim_turned,
    base_ref,
    load_sem,
    piece_sem,
    part_send,
    part_recv,
    share_send,
    share_recv,
    halo_send,
    halo_recv,
):
    n_grid, n_states, tiles, chunk, breadth, nproj, atoms, centre_weight = dims
    cells, depth = v_ref.shape
    breadth_bits, proj_bits = breadth.bit_length() - 1, nproj.bit_length() - 1
    rim = RADIUS * breadth
    piece = chunk // PIECES
    blocks = piece // depth
    slot_rows = PAIR_CAP * nproj
    me_g, me_s = lax.axis_index("grid"), lax.axis_index("states")
    up, down = lax.rem(me_g + 1, n_grid), lax.rem(me_g + n_grid - 1, n_grid)
    holder = me_g // tiles
    partner = me_s + 1 - 2 * lax.rem(me_s, 2)
    twins = [lax.rem(me_s + 2 * d, n_states) for d in range(1, n_states // 2)]

    def outgoing(h, i, s):
        return sendbuf_last.at[i, s] if h == PIECES - 1 else sendbuf.at[h, i, s]

    def incoming(h, o):
        return arrived_last.at[o] if h == PIECES - 1 else arrived.at[h, o]

    piece_loads = [
        pltpu.make_async_copy(
            proj_hbm.at[pl.ds(i * slot_rows, slot_rows), pl.ds(s * chunk + h * piece, piece)],
            outgoing(h, i, s).at[:, pl.ds(0, piece)],
            piece_sem.at[h, i, s],
        )
        for h in range(PIECES)
        for i in range(tiles)
        for s in range(n_states)
    ]
    load_v, load_pot, *load_tables = [
        pltpu.make_async_copy(src, dst, load_sem.at[n])
        for n, (src, dst) in enumerate(
            (
                (v_hbm, v_ref),
                (pot_hbm, pot_ref),
                (inner_h_hbm, inner_h_ref),
                (inner_l_hbm, inner_l_ref),
                (rim_hbm, rim_ref),
                (across_hbm, across_ref),
            )
        )
    ]
    load_v.start()
    for load in piece_loads:
        load.start()
    load_pot.start()
    for load in load_tables:
        load.start()

    barrier = pltpu.get_barrier_semaphore()

    def greet(g, s):
        pl.semaphore_signal(barrier, inc=1, device_id=(g, s), device_id_type=MESH)

    for o in range(n_grid):

        @pl.when((me_g != o) | (holder != me_s))
        def _():
            greet(o, holder)

    greet(up, me_s)
    greet(down, me_s)
    greet(me_g, partner)
    for s in twins:
        greet(me_g, s)

    gain_rows = gain_ref[...]
    nothing = jnp.zeros((slot_rows, depth - nproj), BF16)
    below = jnp.zeros((slot_rows - PAIR_CAP, nproj), BF16)
    for i in range(tiles):
        own_rows = gain_rows[i * PAIR_CAP : (i + 1) * PAIR_CAP]
        block = jnp.concatenate([jnp.concatenate([own_rows, below], axis=0), nothing], axis=1)
        for s in range(n_states):
            sendbuf_last[i, s, :, piece:] = block
    load_v.wait()
    hi_ref[0] = v_ref[...].astype(BF16)
    for load in piece_loads:
        load.wait()

    pl.semaphore_wait(barrier, n_grid + 2 + len(twins) + jnp.where(holder == me_s, 0, 1))

    def part_copy(h, i, d):
        s = lax.rem(me_s + d, n_states)
        return pltpu.make_async_remote_copy(
            src_ref=outgoing(h, i, s),
            dst_ref=incoming(h, me_g),
            send_sem=part_send.at[h, i, d],
            recv_sem=part_recv.at[h, me_g],
            device_id=(me_s * tiles + i, s),
            device_id_type=MESH,
        )

    def halo_copies(step):
        return [
            pltpu.make_async_remote_copy(
                src_ref=hi_ref.at[step, pl.ds(start, rim)],
                dst_ref=halo.at[step, side],
                send_sem=halo_send.at[step, side],
                recv_sem=halo_recv.at[step, side],
                device_id=(target, me_s),
                device_id_type=MESH,
            )
            for side, start, target in ((0, cells - rim, up), (1, 0, down))
        ]

    def share_copy(h, index, part, target):
        return pltpu.make_async_remote_copy(
            src_ref=parts.at[part, h],
            dst_ref=parts.at[part, h],
            send_sem=share_send.at[h, index],
            recv_sem=share_recv.at[h, part],
            device_id=(me_g, target),
            device_id_type=MESH,
        )

    for h in range(PIECES):
        for d in range(n_states - 1, -1, -1):
            for i in range(tiles):
                if d:
                    part_copy(h, i, d).start()
                else:

                    @pl.when(me_s * tiles + i != me_g)
                    def _():
                        part_copy(h, i, 0).start()

                    @pl.when(me_s * tiles + i == me_g)
                    def _():
                        incoming(h, me_g)[...] = outgoing(h, i, me_s)[...]

    for copy in halo_copies(0):
        copy.start()

    owners = [owner_ref[a] for a in range(atoms)]
    slots, ranks = [], []
    for a in range(atoms):
        rank = jnp.int32(0)
        for b in range(a):
            rank = rank + jnp.where(owners[b] == owners[a], 1, 0)
        slots.append(owners[a] * PAIR_CAP + rank)
        ranks.append(rank)
    width = n_grid * slot_rows
    lane = lax.broadcasted_iota(jnp.int32, (nproj, width), 1)
    row = lax.broadcasted_iota(jnp.int32, (nproj, width), 0)
    chosen = jnp.concatenate(
        [jnp.where(lane == slots[a] * nproj + row, 1.0, 0.0) for a in range(atoms)], axis=0
    ).astype(BF16)

    lane = lax.broadcasted_iota(jnp.int32, (1, width), 1)
    places = [owner * slot_rows + rank for owner, rank in zip(owners, ranks)]
    slot_lines = [jnp.where(lane == place, 1.0, 0.0) for place in places]
    slot_lines = jnp.concatenate(
        slot_lines + [jnp.zeros((ATOM_PAD - atoms, width), F32)], axis=0
    ).astype(BF16)
    spread = jnp.where(
        (lax.broadcasted_iota(jnp.int32, (depth, atoms * nproj), 1) & (nproj - 1))
        == lax.broadcasted_iota(jnp.int32, (depth, atoms * nproj), 0),
        1.0,
        0.0,
    ).astype(BF16)

    block_rows = rows_ref.shape[1]
    local = rows_ref[...] - me_g * cells
    local = jnp.concatenate(
        [local, jnp.full((ATOM_PAD - atoms, block_rows), -1, jnp.int32)], axis=0
    )
    line = lax.broadcasted_iota(jnp.int32, (ATOM_PAD, cells), 1)
    pick = jnp.concatenate(
        [jnp.where(local[:, b : b + 1] == line, 1.0, 0.0) for b in range(block_rows)], axis=0
    )
    pick_ref[...] = pick.astype(BF16)

    def own_cells(step, field):
        hi = hi_ref[step]
        lo = (field - hi.astype(F32)).astype(BF16)
        both = jnp.concatenate([hi, lo], axis=1)
        wide = dot(inner_h_ref[...], both)
        total = base_ref[...] * field
        total = total + (wide[:, :depth] + wide[:, depth:] + dot(inner_l_ref[...], hi))
        across = dot(hi, across_ref[...])
        total = total + (across[:, :depth] + across[:, depth:])
        return total + dot(lo, across_ref[:, :depth])

    def rims(step):
        for copy in halo_copies(step):
            copy.wait_recv()
        sums = []
        for side in range(2):
            came = halo[step, side]
            sums.append(dot(rim_turned[side, 0], came) + dot(rim_turned[side, 1], came))
        middle = jnp.zeros((cells - 2 * rim, depth), F32)
        return jnp.concatenate([sums[0], middle, sums[1]], axis=0)

    def nonlocal_part(step, gains):
        picked = dot(pick_ref[...], hi_ref[step]).astype(BF16)
        coefficients = jnp.zeros((ATOM_PAD, atoms * nproj), F32)
        pairs = [(q, h) for q in range(n_states) for h in range(PIECES)]
        for n, (q, h) in enumerate(pairs):
            lines = [
                picked[b * ATOM_PAD : (b + 1) * ATOM_PAD]
                for b in range(n * blocks, (n + 1) * blocks)
            ]
            coefficients = coefficients + lax.dot_general(
                jnp.concatenate(lines, axis=1),
                parts[q, h],
                (((1,), (1,)), ((), ())),
                preferred_element_type=F32,
            )
        atom = lax.broadcasted_iota(jnp.int32, coefficients.shape, 0)
        column = lax.broadcasted_iota(jnp.int32, coefficients.shape, 1)
        scaled = jnp.where((column >> proj_bits) == atom, coefficients * gains, 0.0).astype(BF16)
        pieces = []
        for q, h in pairs:
            projected = dot(scaled, parts[q, h]).astype(BF16)
            pieces += [projected[:, b * depth : (b + 1) * depth] for b in range(blocks)]
        return dot(place_ref[...], jnp.concatenate(pieces, axis=0)) * (1.0 / HALF_WIDTH)

    def forward(h):
        for index, s in enumerate(twins):
            share_copy(h, 0, s, partner).wait_recv()
            share_copy(h, 1 + len(twins) + index, s, partner).start()

    def take_share(h):
        for o in range(n_grid):

            @pl.when((me_g != o) | (holder != me_s))
            def _():
                pltpu.make_async_remote_copy(
                    src_ref=outgoing(h, 0, 0),
                    dst_ref=incoming(h, o),
                    send_sem=part_send.at[h, 0, 0],
                    recv_sem=part_recv.at[h, o],
                    device_id=(o, holder),
                    device_id_type=MESH,
                ).wait_recv()

        last = h == PIECES - 1
        came = arrived_last[:, :, :piece] if last else arrived[h]
        parts[me_s, h] = dot(chosen, came.reshape(width, piece)).astype(BF16)
        for index, s in enumerate(twins):
            share_copy(h, 1 + index, me_s, s).start()
        share_copy(h, 0, me_s, partner).start()

    take_share(0)
    place_ref[...] = pick.T.astype(BF16)
    for h in range(1, PIECES):
        take_share(h)
    load_pot.wait()
    for load in load_tables:
        load.wait()

    turn = wrap_ref[0]
    source = lax.broadcasted_iota(jnp.int32, (rim, rim), 0)
    target = lax.broadcasted_iota(jnp.int32, (rim, rim), 1)
    low_turn = jnp.where(me_g == 0, turn, 0)
    high_turn = jnp.where(me_g == n_grid - 1, breadth - turn, 0)
    for side, shift in ((0, low_turn), (1, high_turn)):
        same_plane = (source >> breadth_bits) == (target >> breadth_bits)
        moved = ((source + shift) & (breadth - 1)) == (target & (breadth - 1))
        permute = jnp.where(same_plane & moved, 1.0, 0.0).astype(BF16)
        for half in range(2):
            rim_turned[side, half] = dot(rim_ref[side, half], permute).astype(BF16)

    base_ref[...] = (pot_ref[...] - CENTER) * (1.0 / HALF_WIDTH) + centre_weight

    for h in range(PIECES - 1):
        forward(h)
    start = v_ref[...]
    first = own_cells(0, start)
    forward(PIECES - 1)
    first = first + rims(0)
    gain_lines = arrived_last[:, :, piece:].reshape(width, depth)
    gains = dot(dot(slot_lines, gain_lines).astype(BF16), spread)
    for h in range(PIECES):
        share_copy(h, 0, partner, partner).wait_recv()
        for s in twins:
            share_copy(h, 0, s + 1 - 2 * lax.rem(s, 2), partner).wait_recv()

    first = first + nonlocal_part(0, gains)
    hi_ref[1] = first.astype(BF16)
    for copy in halo_copies(1):
        copy.start()
    second = own_cells(1, first) + nonlocal_part(1, gains)
    second = 2.0 * (second + rims(1)) - start
    hi_ref[2] = second.astype(BF16)
    for copy in halo_copies(2):
        copy.start()
    last = own_cells(2, second) + nonlocal_part(2, gains)
    out_ref[...] = 2.0 * (last + rims(2)) - first

    for h in range(PIECES):
        for d in range(n_states):
            for i in range(tiles):
                if d:
                    part_copy(h, i, d).wait_send()
                else:

                    @pl.when(me_s * tiles + i != me_g)
                    def _():
                        part_copy(h, i, 0).wait_send()

        share_copy(h, 0, me_s, partner).wait_send()
        for index, s in enumerate(twins):
            share_copy(h, 1 + index, me_s, s).wait_send()
            share_copy(h, 1 + len(twins) + index, s, partner).wait_send()
    for step in range(3):
        for copy in halo_copies(step):
            copy.wait_send()


def shards(states_in, potential, projectors, proj_gains, atom_owner, atom_rows, wrap_rows):
    _, planes, breadth, depth = states_in.shape
    n_grid, n_states = lax.axis_size("grid"), lax.axis_size("states")
    _, held, nproj, span = projectors.shape
    atoms = atom_owner.shape[0]
    cells, rim = planes * breadth, RADIUS * breadth
    tiles = held // PAIR_CAP
    chunk = span // n_states
    piece = chunk // PIECES
    slot_rows = PAIR_CAP * nproj
    inner, low, high, across, centre_weight = stencil_matrices(planes, breadth, depth)
    inner_h, inner_l = halves(inner)
    rim_matrices = np.stack([np.stack(halves(low)), np.stack(halves(high))])
    across_both = np.concatenate(halves(across), axis=1)
    dims = (n_grid, n_states, tiles, chunk, breadth, nproj, atoms, centre_weight)
    hbm = pl.BlockSpec(memory_space=pltpu.HBM)
    vmem = pl.BlockSpec(memory_space=pltpu.VMEM)
    smem = pl.BlockSpec(memory_space=pltpu.SMEM)
    flops = 2 * 3 * depth * cells * (5 * cells + 3 * depth)
    out = pl.pallas_call(
        functools.partial(kernel, dims),
        out_shape=jax.ShapeDtypeStruct((cells, depth), F32),
        in_specs=[hbm] * 7 + [vmem, smem, vmem, smem],
        out_specs=vmem,
        scratch_shapes=[
            pltpu.VMEM((cells, depth), F32),
            pltpu.VMEM((cells, depth), F32),
            pltpu.VMEM((cells, cells), BF16),
            pltpu.VMEM((cells, cells), BF16),
            pltpu.VMEM((2, 2, rim, rim), BF16),
            pltpu.VMEM((depth, 2 * depth), BF16),
            pltpu.VMEM((PIECES - 1, tiles, n_states, slot_rows, piece), BF16),
            pltpu.VMEM((tiles, n_states, slot_rows, piece + depth), BF16),
            pltpu.VMEM((PIECES - 1, n_grid, slot_rows, piece), BF16),
            pltpu.VMEM((n_grid, slot_rows, piece + depth), BF16),
            pltpu.VMEM((n_states, PIECES, atoms * nproj, piece), BF16),
            pltpu.VMEM((3, cells, depth), BF16),
            pltpu.VMEM((3, 2, rim, depth), BF16),
            pltpu.VMEM((ATOM_PAD * atom_rows.shape[1], cells), BF16),
            pltpu.VMEM((cells, ATOM_PAD * atom_rows.shape[1]), BF16),
            pltpu.VMEM((2, 2, rim, rim), BF16),
            pltpu.VMEM((cells, depth), F32),
            pltpu.SemaphoreType.DMA((6,)),
            pltpu.SemaphoreType.DMA((PIECES, tiles, n_states)),
            pltpu.SemaphoreType.DMA((PIECES, tiles, n_states)),
            pltpu.SemaphoreType.DMA((PIECES, n_grid)),
            pltpu.SemaphoreType.DMA((PIECES, n_states)),
            pltpu.SemaphoreType.DMA((PIECES, n_states)),
            pltpu.SemaphoreType.DMA((3, 2)),
            pltpu.SemaphoreType.DMA((3, 2)),
        ],
        compiler_params=pltpu.CompilerParams(
            collective_id=0, has_side_effects=True, vmem_limit_bytes=63 * 1024 * 1024
        ),
        cost_estimate=pl.CostEstimate(
            flops=flops, bytes_accessed=4 * 1024 * 1024, transcendentals=0
        ),
    )(
        states_in.reshape(cells, depth),
        potential.reshape(cells, depth),
        projectors.reshape(held * nproj, span),
        jnp.asarray(inner_h),
        jnp.asarray(inner_l),
        jnp.asarray(rim_matrices),
        jnp.asarray(across_both),
        proj_gains.reshape(held, nproj),
        atom_owner,
        atom_rows,
        wrap_rows,
    )
    return out.reshape(states_in.shape)


def solution(mesh):
    in_specs = (
        P("states", "grid", None, None),
        P("grid", None, None),
        P("grid", "states", None, None),
        P("grid", "states", None),
        P("grid"),
        P("grid", None),
        P(),
    )
    out_specs = P("states", "grid", None, None)
    return jax.shard_map(shards, mesh=mesh, in_specs=in_specs, out_specs=out_specs, check_vma=False)
```

```python
import functools
import math

import jax
import jax.numpy as jnp
import ml_dtypes
import numpy as np
from jax import lax
from jax.experimental import pallas as pl
from jax.experimental.pallas import tpu as pltpu
from jax.sharding import PartitionSpec as P

RADIUS = 6
PAIR_CAP = 2
ATOM_PAD = 16
PIECES = 2

MIXED_WEIGHT = 0.7
CENTER = 12.0
HALF_WIDTH = 8.0

MESH = pl.DeviceIdType.MESH
F32 = jnp.float32
BF16 = jnp.bfloat16


def second_table(radius):
    weights = [-2.0 * sum((1.0 / (k * k) for k in range(1, radius + 1)))]
    for k in range(1, radius + 1):
        weights.append(
            2.0
            * (-1) ** (k + 1)
            * math.factorial(radius) ** 2
            / (k * k * math.factorial(radius - k) * math.factorial(radius + k))
        )
    return weights


def first_table(radius):
    weights = [0.0]
    for k in range(1, radius + 1):
        weights.append(
            (-1) ** (k + 1)
            * math.factorial(radius) ** 2
            / (k * math.factorial(radius - k) * math.factorial(radius + k))
        )
    return weights


def stencil_matrices(planes, breadth, depth):
    second, first = second_table(RADIUS), first_table(RADIUS)
    factor = -0.5 / HALF_WIDTH
    steps = range(1, RADIUS + 1)
    wide = planes + 2 * RADIUS
    lines = np.zeros((planes, breadth, wide, breadth))
    rows = np.arange(breadth)
    for x in range(planes):
        centre = x + RADIUS
        for k in steps:
            for sign in (1, -1):
                lines[x, rows, centre + sign * k, rows] += second[k]
                lines[x, rows, centre, (rows + sign * k) % breadth] += second[k]
                for j in steps:
                    for turn in (1, -1):
                        lines[x, rows, centre + sign * k, (rows + turn * j) % breadth] += (
                            MIXED_WEIGHT * sign * turn * first[k] * first[j]
                        )
    lines = factor * lines.reshape(planes * breadth, wide * breadth)
    across = np.zeros((depth, depth))
    for k in steps:
        across += second[k] * (np.eye(depth, k=k) + np.eye(depth, k=-k))
    rim = RADIUS * breadth
    inner = lines[:, rim:-rim]
    low = lines[:rim, :rim]
    high = lines[-rim:, -rim:]
    return inner, low, high, factor * across, factor * 3.0 * second[0]


def halves(matrix):
    high = matrix.astype(ml_dtypes.bfloat16)
    low = (matrix - high.astype(np.float64)).astype(ml_dtypes.bfloat16)
    return high, low


def dot(a, b):
    return jnp.dot(a, b, preferred_element_type=F32)


def kernel(
    dims,
    v_hbm,
    pot_hbm,
    proj_hbm,
    inner_h_hbm,
    inner_l_hbm,
    rim_hbm,
    across_hbm,
    gain_ref,
    owner_ref,
    rows_ref,
    wrap_ref,
    out_ref,
    v_ref,
    pot_ref,
    inner_h_ref,
    inner_l_ref,
    rim_ref,
    across_ref,
    sendbuf,
    sendbuf_last,
    relay,
    relay_last,
    arrived,
    arrived_last,
    parts,
    hi_ref,
    halo,
    pick_ref,
    place_ref,
    rim_turned,
    base_ref,
    load_sem,
    piece_sem,
    hop_send,
    hop_recv,
    part_send,
    part_recv,
    share_send,
    share_recv,
    halo_send,
    halo_recv,
):
    n_grid, n_states, tiles, chunk, breadth, nproj, atoms, centre_weight = dims
    cells, depth = v_ref.shape
    breadth_bits, proj_bits = breadth.bit_length() - 1, nproj.bit_length() - 1
    rim = RADIUS * breadth
    piece = chunk // PIECES
    blocks = piece // depth
    slot_rows = PAIR_CAP * nproj
    me_g, me_s = lax.axis_index("grid"), lax.axis_index("states")
    up, down = lax.rem(me_g + 1, n_grid), lax.rem(me_g + n_grid - 1, n_grid)
    core = lax.rem(me_s, 2)
    side_x, sides = me_s // 2, n_states // 2
    source_s = 2 * side_x + lax.rem(me_g // tiles, 2)
    others = [lax.rem(side_x + d, sides) for d in range(1, sides)]
    partner = me_s + 1 - 2 * lax.rem(me_s, 2)
    twins = [lax.rem(me_s + 2 * d, n_states) for d in range(1, n_states // 2)]

    def start_copy(copy):
        copy.start()

    def await_sent(copy):
        copy.wait_send()

    def outgoing(h, x):
        return sendbuf_last.at[x] if h == PIECES - 1 else sendbuf.at[h, x]

    def relayed(h, x):
        return relay_last.at[x] if h == PIECES - 1 else relay.at[h, x]

    def incoming(h, o):
        return arrived_last.at[o] if h == PIECES - 1 else arrived.at[h, o]

    piece_loads = [
        pltpu.make_async_copy(
            proj_hbm.at[pl.ds(i * slot_rows, slot_rows), pl.ds(s * chunk + h * piece, piece)],
            outgoing(h, s // 2).at[i, s % 2, :, pl.ds(0, piece)],
            piece_sem.at[h, i, s],
        )
        for h in range(PIECES)
        for i in range(tiles)
        for s in range(n_states)
    ]
    load_v, load_pot, *load_tables = [
        pltpu.make_async_copy(src, dst, load_sem.at[n])
        for n, (src, dst) in enumerate(
            (
                (v_hbm, v_ref),
                (pot_hbm, pot_ref),
                (inner_h_hbm, inner_h_ref),
                (inner_l_hbm, inner_l_ref),
                (rim_hbm, rim_ref),
                (across_hbm, across_ref),
            )
        )
    ]
    load_v.start()
    for load in piece_loads:
        load.start()
    load_pot.start()
    for load in load_tables:
        load.start()

    barrier = pltpu.get_barrier_semaphore()

    def greet(g, s):
        pl.semaphore_signal(barrier, inc=1, device_id=(g, s), device_id_type=MESH)

    for o in range(n_grid):

        @pl.when((me_g != o) | (source_s != me_s))
        def _():
            greet(o, source_s)

    greet(up, me_s)
    greet(down, me_s)
    greet(me_g, partner)
    for s in twins:
        greet(me_g, s)

    gain_rows = gain_ref[...]
    nothing = jnp.zeros((slot_rows, depth - nproj), BF16)
    below = jnp.zeros((slot_rows - PAIR_CAP, nproj), BF16)
    for i in range(tiles):
        own_rows = gain_rows[i * PAIR_CAP : (i + 1) * PAIR_CAP]
        block = jnp.concatenate([jnp.concatenate([own_rows, below], axis=0), nothing], axis=1)
        for s in range(n_states):
            sendbuf_last[s // 2, i, s % 2, :, piece:] = block
    load_v.wait()
    hi_ref[0] = v_ref[...].astype(BF16)
    for load in piece_loads:
        load.wait()

    pl.semaphore_wait(barrier, n_grid + 2 + len(twins) + jnp.where(source_s == me_s, 0, 1))

    def hop_copy(h, d):
        return pltpu.make_async_remote_copy(
            src_ref=outgoing(h, others[d]),
            dst_ref=relayed(h, side_x),
            send_sem=hop_send.at[h, d],
            recv_sem=hop_recv.at[h, side_x],
            device_id=(me_g, 2 * others[d] + core),
            device_id_type=MESH,
        )

    def await_hop(h, d):
        pltpu.make_async_remote_copy(
            src_ref=outgoing(h, others[d]),
            dst_ref=relayed(h, others[d]),
            send_sem=hop_send.at[h, d],
            recv_sem=hop_recv.at[h, others[d]],
            device_id=(me_g, 2 * others[d] + core),
            device_id_type=MESH,
        ).wait_recv()

    def part_copies(h, d, act):
        x = others[d - 1] if d else side_x
        held = relayed(h, x) if d else outgoing(h, x)
        for i in range(tiles):
            tile = (2 * x + core) * tiles + i
            for c in (1, 0):
                copy = pltpu.make_async_remote_copy(
                    src_ref=held.at[i, c],
                    dst_ref=incoming(h, me_g),
                    send_sem=part_send.at[h, d, i, c],
                    recv_sem=part_recv.at[h, me_g],
                    device_id=(tile, 2 * side_x + c),
                    device_id_type=MESH,
                )
                here = (tile == me_g) & (core == c)

                @pl.when(jnp.logical_not(here))
                def _():
                    act(copy)

                if act is start_copy:

                    @pl.when(here)
                    def _():
                        incoming(h, me_g)[...] = held[i, c]

    def halo_copies(step):
        return [
            pltpu.make_async_remote_copy(
                src_ref=hi_ref.at[step, pl.ds(start, rim)],
                dst_ref=halo.at[step, side],
                send_sem=halo_send.at[step, side],
                recv_sem=halo_recv.at[step, side],
                device_id=(target, me_s),
                device_id_type=MESH,
            )
            for side, start, target in ((0, cells - rim, up), (1, 0, down))
        ]

    def share_copy(h, index, part, target):
        return pltpu.make_async_remote_copy(
            src_ref=parts.at[part, h],
            dst_ref=parts.at[part, h],
            send_sem=share_send.at[h, index],
            recv_sem=share_recv.at[h, part],
            device_id=(me_g, target),
            device_id_type=MESH,
        )

    for h in range(PIECES):
        for d in range(sides - 1):
            hop_copy(h, d).start()
        part_copies(h, 0, start_copy)

    owners = [owner_ref[a] for a in range(atoms)]
    slots, ranks = [], []
    for a in range(atoms):
        rank = jnp.int32(0)
        for b in range(a):
            rank = rank + jnp.where(owners[b] == owners[a], 1, 0)
        slots.append(owners[a] * PAIR_CAP + rank)
        ranks.append(rank)
    width = n_grid * slot_rows
    lane = lax.broadcasted_iota(jnp.int32, (nproj, width), 1)
    row = lax.broadcasted_iota(jnp.int32, (nproj, width), 0)
    chosen = jnp.concatenate(
        [jnp.where(lane == slots[a] * nproj + row, 1.0, 0.0) for a in range(atoms)], axis=0
    ).astype(BF16)

    lane = lax.broadcasted_iota(jnp.int32, (1, width), 1)
    places = [owner * slot_rows + rank for owner, rank in zip(owners, ranks)]
    slot_lines = [jnp.where(lane == place, 1.0, 0.0) for place in places]
    slot_lines = jnp.concatenate(
        slot_lines + [jnp.zeros((ATOM_PAD - atoms, width), F32)], axis=0
    ).astype(BF16)
    spread = jnp.where(
        (lax.broadcasted_iota(jnp.int32, (depth, atoms * nproj), 1) & (nproj - 1))
        == lax.broadcasted_iota(jnp.int32, (depth, atoms * nproj), 0),
        1.0,
        0.0,
    ).astype(BF16)

    block_rows = rows_ref.shape[1]
    local = rows_ref[...] - me_g * cells
    local = jnp.concatenate(
        [local, jnp.full((ATOM_PAD - atoms, block_rows), -1, jnp.int32)], axis=0
    )
    line = lax.broadcasted_iota(jnp.int32, (ATOM_PAD, cells), 1)
    pick = jnp.concatenate(
        [jnp.where(local[:, b : b + 1] == line, 1.0, 0.0) for b in range(block_rows)], axis=0
    )
    pick_ref[...] = pick.astype(BF16)

    for h in range(PIECES):
        for d in range(sides - 1):
            await_hop(h, d)
            part_copies(h, d + 1, start_copy)
    for copy in halo_copies(0):
        copy.start()


    def own_cells(step, field):
        hi = hi_ref[step]
        lo = (field - hi.astype(F32)).astype(BF16)
        both = jnp.concatenate([hi, lo], axis=1)
        wide = dot(inner_h_ref[...], both)
        total = base_ref[...] * field
        total = total + (wide[:, :depth] + wide[:, depth:] + dot(inner_l_ref[...], hi))
        across = dot(hi, across_ref[...])
        total = total + (across[:, :depth] + across[:, depth:])
        return total + dot(lo, across_ref[:, :depth])

    def rims(step):
        for copy in halo_copies(step):
            copy.wait_recv()
        sums = []
        for side in range(2):
            came = halo[step, side]
            sums.append(dot(rim_turned[side, 0], came) + dot(rim_turned[side, 1], came))
        middle = jnp.zeros((cells - 2 * rim, depth), F32)
        return jnp.concatenate([sums[0], middle, sums[1]], axis=0)

    def nonlocal_part(step, gains):
        picked = dot(pick_ref[...], hi_ref[step]).astype(BF16)
        coefficients = jnp.zeros((ATOM_PAD, atoms * nproj), F32)
        pairs = [(q, h) for q in range(n_states) for h in range(PIECES)]
        for n, (q, h) in enumerate(pairs):
            lines = [
                picked[b * ATOM_PAD : (b + 1) * ATOM_PAD]
                for b in range(n * blocks, (n + 1) * blocks)
            ]
            coefficients = coefficients + lax.dot_general(
                jnp.concatenate(lines, axis=1),
                parts[q, h],
                (((1,), (1,)), ((), ())),
                preferred_element_type=F32,
            )
        atom = lax.broadcasted_iota(jnp.int32, coefficients.shape, 0)
        column = lax.broadcasted_iota(jnp.int32, coefficients.shape, 1)
        scaled = jnp.where((column >> proj_bits) == atom, coefficients * gains, 0.0).astype(BF16)
        pieces = []
        for q, h in pairs:
            projected = dot(scaled, parts[q, h]).astype(BF16)
            pieces += [projected[:, b * depth : (b + 1) * depth] for b in range(blocks)]
        return dot(place_ref[...], jnp.concatenate(pieces, axis=0)) * (1.0 / HALF_WIDTH)

    def forward(h):
        for index, s in enumerate(twins):
            share_copy(h, 0, s, partner).wait_recv()
            share_copy(h, 1 + len(twins) + index, s, partner).start()

    def take_share(h):
        for o in range(n_grid):

            @pl.when((me_g != o) | (source_s != me_s))
            def _():
                pltpu.make_async_remote_copy(
                    src_ref=outgoing(h, 0).at[0, 0],
                    dst_ref=incoming(h, o),
                    send_sem=part_send.at[h, 0, 0, 0],
                    recv_sem=part_recv.at[h, o],
                    device_id=(o, source_s),
                    device_id_type=MESH,
                ).wait_recv()

        last = h == PIECES - 1
        came = arrived_last[:, :, :piece] if last else arrived[h]
        parts[me_s, h] = dot(chosen, came.reshape(width, piece)).astype(BF16)
        for index, s in enumerate(twins):
            share_copy(h, 1 + index, me_s, s).start()
        share_copy(h, 0, me_s, partner).start()

    take_share(0)
    place_ref[...] = pick.T.astype(BF16)
    for h in range(1, PIECES):
        take_share(h)
    load_pot.wait()
    for load in load_tables:
        load.wait()

    turn = wrap_ref[0]
    source = lax.broadcasted_iota(jnp.int32, (rim, rim), 0)
    target = lax.broadcasted_iota(jnp.int32, (rim, rim), 1)
    low_turn = jnp.where(me_g == 0, turn, 0)
    high_turn = jnp.where(me_g == n_grid - 1, breadth - turn, 0)
    for side, shift in ((0, low_turn), (1, high_turn)):
        same_plane = (source >> breadth_bits) == (target >> breadth_bits)
        moved = ((source + shift) & (breadth - 1)) == (target & (breadth - 1))
        permute = jnp.where(same_plane & moved, 1.0, 0.0).astype(BF16)
        for half in range(2):
            rim_turned[side, half] = dot(rim_ref[side, half], permute).astype(BF16)

    base_ref[...] = (pot_ref[...] - CENTER) * (1.0 / HALF_WIDTH) + centre_weight

    for h in range(PIECES - 1):
        forward(h)
    start = v_ref[...]
    first = own_cells(0, start)
    forward(PIECES - 1)
    first = first + rims(0)
    gain_lines = arrived_last[:, :, piece:].reshape(width, depth)
    gains = dot(dot(slot_lines, gain_lines).astype(BF16), spread)
    for h in range(PIECES):
        share_copy(h, 0, partner, partner).wait_recv()
        for s in twins:
            share_copy(h, 0, s + 1 - 2 * lax.rem(s, 2), partner).wait_recv()

    first = first + nonlocal_part(0, gains)
    hi_ref[1] = first.astype(BF16)
    for copy in halo_copies(1):
        copy.start()
    second = own_cells(1, first) + nonlocal_part(1, gains)
    second = 2.0 * (second + rims(1)) - start
    hi_ref[2] = second.astype(BF16)
    for copy in halo_copies(2):
        copy.start()
    last = own_cells(2, second) + nonlocal_part(2, gains)
    out_ref[...] = 2.0 * (last + rims(2)) - first

    for h in range(PIECES):
        for d in range(sides - 1):
            hop_copy(h, d).wait_send()
        for d in range(sides):
            part_copies(h, d, await_sent)
        share_copy(h, 0, me_s, partner).wait_send()
        for index, s in enumerate(twins):
            share_copy(h, 1 + index, me_s, s).wait_send()
            share_copy(h, 1 + len(twins) + index, s, partner).wait_send()
    for step in range(3):
        for copy in halo_copies(step):
            copy.wait_send()


def shards(states_in, potential, projectors, proj_gains, atom_owner, atom_rows, wrap_rows):
    _, planes, breadth, depth = states_in.shape
    n_grid, n_states = lax.axis_size("grid"), lax.axis_size("states")
    _, held, nproj, span = projectors.shape
    atoms = atom_owner.shape[0]
    cells, rim = planes * breadth, RADIUS * breadth
    tiles = held // PAIR_CAP
    chunk = span // n_states
    piece, sides = chunk // PIECES, n_states // 2
    slot_rows = PAIR_CAP * nproj
    inner, low, high, across, centre_weight = stencil_matrices(planes, breadth, depth)
    inner_h, inner_l = halves(inner)
    rim_matrices = np.stack([np.stack(halves(low)), np.stack(halves(high))])
    across_both = np.concatenate(halves(across), axis=1)
    dims = (n_grid, n_states, tiles, chunk, breadth, nproj, atoms, centre_weight)
    hbm = pl.BlockSpec(memory_space=pltpu.HBM)
    vmem = pl.BlockSpec(memory_space=pltpu.VMEM)
    smem = pl.BlockSpec(memory_space=pltpu.SMEM)
    flops = 2 * 3 * depth * cells * (5 * cells + 3 * depth)
    out = pl.pallas_call(
        functools.partial(kernel, dims),
        out_shape=jax.ShapeDtypeStruct((cells, depth), F32),
        in_specs=[hbm] * 7 + [vmem, smem, vmem, smem],
        out_specs=vmem,
        scratch_shapes=[
            pltpu.VMEM((cells, depth), F32),
            pltpu.VMEM((cells, depth), F32),
            pltpu.VMEM((cells, cells), BF16),
            pltpu.VMEM((cells, cells), BF16),
            pltpu.VMEM((2, 2, rim, rim), BF16),
            pltpu.VMEM((depth, 2 * depth), BF16),
            pltpu.VMEM((PIECES - 1, sides, tiles, 2, slot_rows, piece), BF16),
            pltpu.VMEM((sides, tiles, 2, slot_rows, piece + depth), BF16),
            pltpu.VMEM((PIECES - 1, sides, tiles, 2, slot_rows, piece), BF16),
            pltpu.VMEM((sides, tiles, 2, slot_rows, piece + depth), BF16),
            pltpu.VMEM((PIECES - 1, n_grid, slot_rows, piece), BF16),
            pltpu.VMEM((n_grid, slot_rows, piece + depth), BF16),
            pltpu.VMEM((n_states, PIECES, atoms * nproj, piece), BF16),
            pltpu.VMEM((3, cells, depth), BF16),
            pltpu.VMEM((3, 2, rim, depth), BF16),
            pltpu.VMEM((ATOM_PAD * atom_rows.shape[1], cells), BF16),
            pltpu.VMEM((cells, ATOM_PAD * atom_rows.shape[1]), BF16),
            pltpu.VMEM((2, 2, rim, rim), BF16),
            pltpu.VMEM((cells, depth), F32),
            pltpu.SemaphoreType.DMA((6,)),
            pltpu.SemaphoreType.DMA((PIECES, tiles, n_states)),
            pltpu.SemaphoreType.DMA((PIECES, sides)),
            pltpu.SemaphoreType.DMA((PIECES, sides)),
            pltpu.SemaphoreType.DMA((PIECES, sides, tiles, 2)),
            pltpu.SemaphoreType.DMA((PIECES, n_grid)),
            pltpu.SemaphoreType.DMA((PIECES, n_states)),
            pltpu.SemaphoreType.DMA((PIECES, n_states)),
            pltpu.SemaphoreType.DMA((3, 2)),
            pltpu.SemaphoreType.DMA((3, 2)),
        ],
        compiler_params=pltpu.CompilerParams(
            collective_id=0, has_side_effects=True, vmem_limit_bytes=63 * 1024 * 1024
        ),
        cost_estimate=pl.CostEstimate(
            flops=flops, bytes_accessed=4 * 1024 * 1024, transcendentals=0
        ),
    )(
        states_in.reshape(cells, depth),
        potential.reshape(cells, depth),
        projectors.reshape(held * nproj, span),
        jnp.asarray(inner_h),
        jnp.asarray(inner_l),
        jnp.asarray(rim_matrices),
        jnp.asarray(across_both),
        proj_gains.reshape(held, nproj),
        atom_owner,
        atom_rows,
        wrap_rows,
    )
    return out.reshape(states_in.shape)


def solution(mesh):
    in_specs = (
        P("states", "grid", None, None),
        P("grid", None, None),
        P("grid", "states", None, None),
        P("grid", "states", None),
        P("grid"),
        P("grid", None),
        P(),
    )
    out_specs = P("states", "grid", None, None)
    return jax.shard_map(shards, mesh=mesh, in_specs=in_specs, out_specs=out_specs, check_vma=False)
```

```python
import functools
import math

import jax
import jax.numpy as jnp
import ml_dtypes
import numpy as np
from jax import lax
from jax.experimental import pallas as pl
from jax.experimental.pallas import tpu as pltpu
from jax.sharding import PartitionSpec as P

RADIUS = 6
PAIR_CAP = 2
ATOM_PAD = 16
MOST_PIECES = 4

MIXED_WEIGHT = 0.7
CENTER = 12.0
HALF_WIDTH = 8.0

MESH = pl.DeviceIdType.MESH
F32 = jnp.float32
BF16 = jnp.bfloat16


def second_table(radius):
    weights = [-2.0 * sum((1.0 / (k * k) for k in range(1, radius + 1)))]
    for k in range(1, radius + 1):
        weights.append(
            2.0
            * (-1) ** (k + 1)
            * math.factorial(radius) ** 2
            / (k * k * math.factorial(radius - k) * math.factorial(radius + k))
        )
    return weights


def first_table(radius):
    weights = [0.0]
    for k in range(1, radius + 1):
        weights.append(
            (-1) ** (k + 1)
            * math.factorial(radius) ** 2
            / (k * math.factorial(radius - k) * math.factorial(radius + k))
        )
    return weights


def stencil_matrices(planes, breadth, depth):
    second, first = second_table(RADIUS), first_table(RADIUS)
    factor = -0.5 / HALF_WIDTH
    steps = range(1, RADIUS + 1)
    wide = planes + 2 * RADIUS
    lines = np.zeros((planes, breadth, wide, breadth))
    rows = np.arange(breadth)
    for x in range(planes):
        centre = x + RADIUS
        for k in steps:
            for sign in (1, -1):
                lines[x, rows, centre + sign * k, rows] += second[k]
                lines[x, rows, centre, (rows + sign * k) % breadth] += second[k]
                for j in steps:
                    for turn in (1, -1):
                        lines[x, rows, centre + sign * k, (rows + turn * j) % breadth] += (
                            MIXED_WEIGHT * sign * turn * first[k] * first[j]
                        )
    lines = factor * lines.reshape(planes * breadth, wide * breadth)
    across = np.zeros((depth, depth))
    for k in steps:
        across += second[k] * (np.eye(depth, k=k) + np.eye(depth, k=-k))
    rim = RADIUS * breadth
    inner = lines[:, rim:-rim]
    low = lines[:rim, :rim]
    high = lines[-rim:, -rim:]
    return inner, low, high, factor * across, factor * 3.0 * second[0]


def halves(matrix):
    high = matrix.astype(ml_dtypes.bfloat16)
    low = (matrix - high.astype(np.float64)).astype(ml_dtypes.bfloat16)
    return high, low


def dot(a, b):
    return jnp.dot(a, b, preferred_element_type=F32)


def kernel(
    dims,
    v_hbm,
    pot_hbm,
    proj_hbm,
    inner_h_hbm,
    inner_l_hbm,
    rim_hbm,
    across_hbm,
    gain_ref,
    owner_ref,
    rows_ref,
    wrap_ref,
    out_ref,
    v_ref,
    pot_ref,
    inner_h_ref,
    inner_l_ref,
    rim_ref,
    across_ref,
    sendbuf,
    sendbuf_last,
    relay,
    relay_last,
    arrived,
    arrived_last,
    parts,
    hi_ref,
    halo,
    pick_ref,
    place_ref,
    rim_turned,
    base_ref,
    load_sem,
    piece_sem,
    hop_send,
    hop_recv,
    part_send,
    part_recv,
    share_send,
    share_recv,
    halo_send,
    halo_recv,
):
    n_grid, n_states, tiles, chunk, breadth, nproj, atoms, centre_weight = dims
    cells, depth = v_ref.shape
    breadth_bits, proj_bits = breadth.bit_length() - 1, nproj.bit_length() - 1
    rim = RADIUS * breadth
    count = min(MOST_PIECES, chunk // depth)
    piece = chunk // count
    blocks = piece // depth
    slot_rows = PAIR_CAP * nproj
    me_g, me_s = lax.axis_index("grid"), lax.axis_index("states")
    up, down = lax.rem(me_g + 1, n_grid), lax.rem(me_g + n_grid - 1, n_grid)
    core = lax.rem(me_s, 2)
    side_x, sides = me_s // 2, n_states // 2
    source_s = 2 * side_x + lax.rem(me_g // tiles, 2)
    others = [lax.rem(side_x + d, sides) for d in range(1, sides)]
    partner = me_s + 1 - 2 * lax.rem(me_s, 2)
    twins = [lax.rem(me_s + 2 * d, n_states) for d in range(1, n_states // 2)]

    def start_copy(copy):
        copy.start()

    def await_sent(copy):
        copy.wait_send()

    def outgoing(h, x):
        return sendbuf_last.at[x] if h == count - 1 else sendbuf.at[h, x]

    def relayed(h, x):
        return relay_last.at[x] if h == count - 1 else relay.at[h, x]

    def incoming(h, o):
        return arrived_last.at[o] if h == count - 1 else arrived.at[h, o]

    piece_loads = [
        pltpu.make_async_copy(
            proj_hbm.at[pl.ds(i * slot_rows, slot_rows), pl.ds(s * chunk + h * piece, piece)],
            outgoing(h, s // 2).at[i, s % 2, :, pl.ds(0, piece)],
            piece_sem.at[h, i, s],
        )
        for h in range(count)
        for i in range(tiles)
        for s in range(n_states)
    ]
    load_v, load_pot, *load_tables = [
        pltpu.make_async_copy(src, dst, load_sem.at[n])
        for n, (src, dst) in enumerate(
            (
                (v_hbm, v_ref),
                (pot_hbm, pot_ref),
                (inner_h_hbm, inner_h_ref),
                (inner_l_hbm, inner_l_ref),
                (rim_hbm, rim_ref),
                (across_hbm, across_ref),
            )
        )
    ]
    load_v.start()
    for load in piece_loads:
        load.start()
    load_pot.start()
    for load in load_tables:
        load.start()

    barrier = pltpu.get_barrier_semaphore()

    def greet(g, s):
        pl.semaphore_signal(barrier, inc=1, device_id=(g, s), device_id_type=MESH)

    for o in range(n_grid):

        @pl.when((me_g != o) | (source_s != me_s))
        def _():
            greet(o, source_s)

    greet(up, me_s)
    greet(down, me_s)
    greet(me_g, partner)
    for s in twins:
        greet(me_g, s)

    gain_rows = gain_ref[...]
    nothing = jnp.zeros((slot_rows, depth - nproj), BF16)
    below = jnp.zeros((slot_rows - PAIR_CAP, nproj), BF16)
    for i in range(tiles):
        own_rows = gain_rows[i * PAIR_CAP : (i + 1) * PAIR_CAP]
        block = jnp.concatenate([jnp.concatenate([own_rows, below], axis=0), nothing], axis=1)
        for s in range(n_states):
            sendbuf_last[s // 2, i, s % 2, :, piece:] = block
    load_v.wait()
    hi_ref[0] = v_ref[...].astype(BF16)
    for load in piece_loads:
        load.wait()

    pl.semaphore_wait(barrier, n_grid + 2 + len(twins) + jnp.where(source_s == me_s, 0, 1))

    def hop_copy(h, d):
        return pltpu.make_async_remote_copy(
            src_ref=outgoing(h, others[d]),
            dst_ref=relayed(h, side_x),
            send_sem=hop_send.at[h, d],
            recv_sem=hop_recv.at[h, side_x],
            device_id=(me_g, 2 * others[d] + core),
            device_id_type=MESH,
        )

    def await_hop(h, d):
        pltpu.make_async_remote_copy(
            src_ref=outgoing(h, others[d]),
            dst_ref=relayed(h, others[d]),
            send_sem=hop_send.at[h, d],
            recv_sem=hop_recv.at[h, others[d]],
            device_id=(me_g, 2 * others[d] + core),
            device_id_type=MESH,
        ).wait_recv()

    def part_copies(h, d, act):
        x = others[d - 1] if d else side_x
        held = relayed(h, x) if d else outgoing(h, x)
        for i in range(tiles):
            tile = (2 * x + core) * tiles + i
            for c in (1, 0):
                copy = pltpu.make_async_remote_copy(
                    src_ref=held.at[i, c],
                    dst_ref=incoming(h, me_g),
                    send_sem=part_send.at[h, d, i, c],
                    recv_sem=part_recv.at[h, me_g],
                    device_id=(tile, 2 * side_x + c),
                    device_id_type=MESH,
                )
                here = (tile == me_g) & (core == c)

                @pl.when(jnp.logical_not(here))
                def _():
                    act(copy)

                if act is start_copy:

                    @pl.when(here)
                    def _():
                        incoming(h, me_g)[...] = held[i, c]

    def halo_copies(step):
        return [
            pltpu.make_async_remote_copy(
                src_ref=hi_ref.at[step, pl.ds(start, rim)],
                dst_ref=halo.at[step, side],
                send_sem=halo_send.at[step, side],
                recv_sem=halo_recv.at[step, side],
                device_id=(target, me_s),
                device_id_type=MESH,
            )
            for side, start, target in ((0, cells - rim, up), (1, 0, down))
        ]

    def share_copy(h, index, part, target):
        return pltpu.make_async_remote_copy(
            src_ref=parts.at[part, h],
            dst_ref=parts.at[part, h],
            send_sem=share_send.at[h, index],
            recv_sem=share_recv.at[h, part],
            device_id=(me_g, target),
            device_id_type=MESH,
        )

    for h in range(count):
        for d in range(sides - 1):
            hop_copy(h, d).start()
        if h < 2:
            part_copies(h, 0, start_copy)

    def forward_parts(h):
        for d in range(sides - 1):
            await_hop(h, d)
            part_copies(h, d + 1, start_copy)
        if h + 2 < count:
            part_copies(h + 2, 0, start_copy)

    owners = [owner_ref[a] for a in range(atoms)]
    slots, ranks = [], []
    for a in range(atoms):
        rank = jnp.int32(0)
        for b in range(a):
            rank = rank + jnp.where(owners[b] == owners[a], 1, 0)
        slots.append(owners[a] * PAIR_CAP + rank)
        ranks.append(rank)
    width = n_grid * slot_rows
    lane = lax.broadcasted_iota(jnp.int32, (nproj, width), 1)
    row = lax.broadcasted_iota(jnp.int32, (nproj, width), 0)
    chosen = jnp.concatenate(
        [jnp.where(lane == slots[a] * nproj + row, 1.0, 0.0) for a in range(atoms)], axis=0
    ).astype(BF16)

    lane = lax.broadcasted_iota(jnp.int32, (1, width), 1)
    places = [owner * slot_rows + rank for owner, rank in zip(owners, ranks)]
    slot_lines = [jnp.where(lane == place, 1.0, 0.0) for place in places]
    slot_lines = jnp.concatenate(
        slot_lines + [jnp.zeros((ATOM_PAD - atoms, width), F32)], axis=0
    ).astype(BF16)
    spread = jnp.where(
        (lax.broadcasted_iota(jnp.int32, (depth, atoms * nproj), 1) & (nproj - 1))
        == lax.broadcasted_iota(jnp.int32, (depth, atoms * nproj), 0),
        1.0,
        0.0,
    ).astype(BF16)

    forward_parts(0)
    block_rows = rows_ref.shape[1]
    local = rows_ref[...] - me_g * cells
    local = jnp.concatenate(
        [local, jnp.full((ATOM_PAD - atoms, block_rows), -1, jnp.int32)], axis=0
    )
    line = lax.broadcasted_iota(jnp.int32, (ATOM_PAD, cells), 1)
    pick = jnp.concatenate(
        [jnp.where(local[:, b : b + 1] == line, 1.0, 0.0) for b in range(block_rows)], axis=0
    )
    pick_ref[...] = pick.astype(BF16)


    def own_cells(step, field):
        hi = hi_ref[step]
        lo = (field - hi.astype(F32)).astype(BF16)
        both = jnp.concatenate([hi, lo], axis=1)
        wide = dot(inner_h_ref[...], both)
        total = base_ref[...] * field
        total = total + (wide[:, :depth] + wide[:, depth:] + dot(inner_l_ref[...], hi))
        across = dot(hi, across_ref[...])
        total = total + (across[:, :depth] + across[:, depth:])
        return total + dot(lo, across_ref[:, :depth])

    def rims(step):
        for copy in halo_copies(step):
            copy.wait_recv()
        sums = []
        for side in range(2):
            came = halo[step, side]
            sums.append(dot(rim_turned[side, 0], came) + dot(rim_turned[side, 1], came))
        middle = jnp.zeros((cells - 2 * rim, depth), F32)
        return jnp.concatenate([sums[0], middle, sums[1]], axis=0)

    def nonlocal_part(step, gains):
        picked = dot(pick_ref[...], hi_ref[step]).astype(BF16)
        coefficients = jnp.zeros((ATOM_PAD, atoms * nproj), F32)
        pairs = [(q, h) for q in range(n_states) for h in range(count)]
        for n, (q, h) in enumerate(pairs):
            lines = [
                picked[b * ATOM_PAD : (b + 1) * ATOM_PAD]
                for b in range(n * blocks, (n + 1) * blocks)
            ]
            coefficients = coefficients + lax.dot_general(
                jnp.concatenate(lines, axis=1),
                parts[q, h],
                (((1,), (1,)), ((), ())),
                preferred_element_type=F32,
            )
        atom = lax.broadcasted_iota(jnp.int32, coefficients.shape, 0)
        column = lax.broadcasted_iota(jnp.int32, coefficients.shape, 1)
        scaled = jnp.where((column >> proj_bits) == atom, coefficients * gains, 0.0).astype(BF16)
        pieces = []
        for q, h in pairs:
            projected = dot(scaled, parts[q, h]).astype(BF16)
            pieces += [projected[:, b * depth : (b + 1) * depth] for b in range(blocks)]
        return dot(place_ref[...], jnp.concatenate(pieces, axis=0)) * (1.0 / HALF_WIDTH)

    def forward(h):
        for index, s in enumerate(twins):
            share_copy(h, 0, s, partner).wait_recv()
            share_copy(h, 1 + len(twins) + index, s, partner).start()

    def take_share(h):
        for o in range(n_grid):

            @pl.when((me_g != o) | (source_s != me_s))
            def _():
                pltpu.make_async_remote_copy(
                    src_ref=outgoing(h, 0).at[0, 0],
                    dst_ref=incoming(h, o),
                    send_sem=part_send.at[h, 0, 0, 0],
                    recv_sem=part_recv.at[h, o],
                    device_id=(o, source_s),
                    device_id_type=MESH,
                ).wait_recv()

        last = h == count - 1
        came = arrived_last[:, :, :piece] if last else arrived[h]
        parts[me_s, h] = dot(chosen, came.reshape(width, piece)).astype(BF16)
        for index, s in enumerate(twins):
            share_copy(h, 1 + index, me_s, s).start()
        share_copy(h, 0, me_s, partner).start()

    for h in range(1, count):
        forward_parts(h)
        if h >= 2:
            take_share(h - 2)
    for copy in halo_copies(0):
        copy.start()
    place_ref[...] = pick.T.astype(BF16)
    for h in range(max(count - 2, 0), count):
        take_share(h)
    load_pot.wait()
    for load in load_tables:
        load.wait()

    turn = wrap_ref[0]
    source = lax.broadcasted_iota(jnp.int32, (rim, rim), 0)
    target = lax.broadcasted_iota(jnp.int32, (rim, rim), 1)
    low_turn = jnp.where(me_g == 0, turn, 0)
    high_turn = jnp.where(me_g == n_grid - 1, breadth - turn, 0)
    for side, shift in ((0, low_turn), (1, high_turn)):
        same_plane = (source >> breadth_bits) == (target >> breadth_bits)
        moved = ((source + shift) & (breadth - 1)) == (target & (breadth - 1))
        permute = jnp.where(same_plane & moved, 1.0, 0.0).astype(BF16)
        for half in range(2):
            rim_turned[side, half] = dot(rim_ref[side, half], permute).astype(BF16)

    base_ref[...] = (pot_ref[...] - CENTER) * (1.0 / HALF_WIDTH) + centre_weight

    for h in range(count - 1):
        forward(h)
    start = v_ref[...]
    first = own_cells(0, start)
    forward(count - 1)
    first = first + rims(0)
    gain_lines = arrived_last[:, :, piece:].reshape(width, depth)
    gains = dot(dot(slot_lines, gain_lines).astype(BF16), spread)
    for h in range(count):
        share_copy(h, 0, partner, partner).wait_recv()
        for s in twins:
            share_copy(h, 0, s + 1 - 2 * lax.rem(s, 2), partner).wait_recv()

    first = first + nonlocal_part(0, gains)
    hi_ref[1] = first.astype(BF16)
    for copy in halo_copies(1):
        copy.start()
    second = own_cells(1, first) + nonlocal_part(1, gains)
    second = 2.0 * (second + rims(1)) - start
    hi_ref[2] = second.astype(BF16)
    for copy in halo_copies(2):
        copy.start()
    last = own_cells(2, second) + nonlocal_part(2, gains)
    out_ref[...] = 2.0 * (last + rims(2)) - first

    for h in range(count):
        for d in range(sides - 1):
            hop_copy(h, d).wait_send()
        for d in range(sides):
            part_copies(h, d, await_sent)
        share_copy(h, 0, me_s, partner).wait_send()
        for index, s in enumerate(twins):
            share_copy(h, 1 + index, me_s, s).wait_send()
            share_copy(h, 1 + len(twins) + index, s, partner).wait_send()
    for step in range(3):
        for copy in halo_copies(step):
            copy.wait_send()


def shards(states_in, potential, projectors, proj_gains, atom_owner, atom_rows, wrap_rows):
    _, planes, breadth, depth = states_in.shape
    n_grid, n_states = lax.axis_size("grid"), lax.axis_size("states")
    _, held, nproj, span = projectors.shape
    atoms = atom_owner.shape[0]
    cells, rim = planes * breadth, RADIUS * breadth
    tiles = held // PAIR_CAP
    chunk = span // n_states
    count = min(MOST_PIECES, chunk // depth)
    piece, sides = chunk // count, n_states // 2
    slot_rows = PAIR_CAP * nproj
    inner, low, high, across, centre_weight = stencil_matrices(planes, breadth, depth)
    inner_h, inner_l = halves(inner)
    rim_matrices = np.stack([np.stack(halves(low)), np.stack(halves(high))])
    across_both = np.concatenate(halves(across), axis=1)
    dims = (n_grid, n_states, tiles, chunk, breadth, nproj, atoms, centre_weight)
    hbm = pl.BlockSpec(memory_space=pltpu.HBM)
    vmem = pl.BlockSpec(memory_space=pltpu.VMEM)
    smem = pl.BlockSpec(memory_space=pltpu.SMEM)
    flops = 2 * 3 * depth * cells * (5 * cells + 3 * depth)
    out = pl.pallas_call(
        functools.partial(kernel, dims),
        out_shape=jax.ShapeDtypeStruct((cells, depth), F32),
        in_specs=[hbm] * 7 + [vmem, smem, vmem, smem],
        out_specs=vmem,
        scratch_shapes=[
            pltpu.VMEM((cells, depth), F32),
            pltpu.VMEM((cells, depth), F32),
            pltpu.VMEM((cells, cells), BF16),
            pltpu.VMEM((cells, cells), BF16),
            pltpu.VMEM((2, 2, rim, rim), BF16),
            pltpu.VMEM((depth, 2 * depth), BF16),
            pltpu.VMEM((count - 1, sides, tiles, 2, slot_rows, piece), BF16),
            pltpu.VMEM((sides, tiles, 2, slot_rows, piece + depth), BF16),
            pltpu.VMEM((count - 1, sides, tiles, 2, slot_rows, piece), BF16),
            pltpu.VMEM((sides, tiles, 2, slot_rows, piece + depth), BF16),
            pltpu.VMEM((count - 1, n_grid, slot_rows, piece), BF16),
            pltpu.VMEM((n_grid, slot_rows, piece + depth), BF16),
            pltpu.VMEM((n_states, count, atoms * nproj, piece), BF16),
            pltpu.VMEM((3, cells, depth), BF16),
            pltpu.VMEM((3, 2, rim, depth), BF16),
            pltpu.VMEM((ATOM_PAD * atom_rows.shape[1], cells), BF16),
            pltpu.VMEM((cells, ATOM_PAD * atom_rows.shape[1]), BF16),
            pltpu.VMEM((2, 2, rim, rim), BF16),
            pltpu.VMEM((cells, depth), F32),
            pltpu.SemaphoreType.DMA((6,)),
            pltpu.SemaphoreType.DMA((count, tiles, n_states)),
            pltpu.SemaphoreType.DMA((count, sides)),
            pltpu.SemaphoreType.DMA((count, sides)),
            pltpu.SemaphoreType.DMA((count, sides, tiles, 2)),
            pltpu.SemaphoreType.DMA((count, n_grid)),
            pltpu.SemaphoreType.DMA((count, n_states)),
            pltpu.SemaphoreType.DMA((count, n_states)),
            pltpu.SemaphoreType.DMA((3, 2)),
            pltpu.SemaphoreType.DMA((3, 2)),
        ],
        compiler_params=pltpu.CompilerParams(
            collective_id=0, has_side_effects=True, vmem_limit_bytes=63 * 1024 * 1024
        ),
        cost_estimate=pl.CostEstimate(
            flops=flops, bytes_accessed=4 * 1024 * 1024, transcendentals=0
        ),
    )(
        states_in.reshape(cells, depth),
        potential.reshape(cells, depth),
        projectors.reshape(held * nproj, span),
        jnp.asarray(inner_h),
        jnp.asarray(inner_l),
        jnp.asarray(rim_matrices),
        jnp.asarray(across_both),
        proj_gains.reshape(held, nproj),
        atom_owner,
        atom_rows,
        wrap_rows,
    )
    return out.reshape(states_in.shape)


def solution(mesh):
    in_specs = (
        P("states", "grid", None, None),
        P("grid", None, None),
        P("grid", "states", None, None),
        P("grid", "states", None),
        P("grid"),
        P("grid", None),
        P(),
    )
    out_specs = P("states", "grid", None, None)
    return jax.shard_map(shards, mesh=mesh, in_specs=in_specs, out_specs=out_specs, check_vma=False)
```

```python
import functools
import math

import jax
import jax.numpy as jnp
import ml_dtypes
import numpy as np
from jax import lax
from jax.experimental import pallas as pl
from jax.experimental.pallas import tpu as pltpu
from jax.sharding import PartitionSpec as P

RADIUS = 6
PAIR_CAP = 2
ATOM_PAD = 16
MOST_PIECES = 4

MIXED_WEIGHT = 0.7
CENTER = 12.0
HALF_WIDTH = 8.0

MESH = pl.DeviceIdType.MESH
F32 = jnp.float32
BF16 = jnp.bfloat16


def second_table(radius):
    weights = [-2.0 * sum((1.0 / (k * k) for k in range(1, radius + 1)))]
    for k in range(1, radius + 1):
        weights.append(
            2.0
            * (-1) ** (k + 1)
            * math.factorial(radius) ** 2
            / (k * k * math.factorial(radius - k) * math.factorial(radius + k))
        )
    return weights


def first_table(radius):
    weights = [0.0]
    for k in range(1, radius + 1):
        weights.append(
            (-1) ** (k + 1)
            * math.factorial(radius) ** 2
            / (k * math.factorial(radius - k) * math.factorial(radius + k))
        )
    return weights


def stencil_matrices(planes, breadth, depth):
    second, first = second_table(RADIUS), first_table(RADIUS)
    factor = -0.5 / HALF_WIDTH
    steps = range(1, RADIUS + 1)
    wide = planes + 2 * RADIUS
    lines = np.zeros((planes, breadth, wide, breadth))
    rows = np.arange(breadth)
    for x in range(planes):
        centre = x + RADIUS
        for k in steps:
            for sign in (1, -1):
                lines[x, rows, centre + sign * k, rows] += second[k]
                lines[x, rows, centre, (rows + sign * k) % breadth] += second[k]
                for j in steps:
                    for turn in (1, -1):
                        lines[x, rows, centre + sign * k, (rows + turn * j) % breadth] += (
                            MIXED_WEIGHT * sign * turn * first[k] * first[j]
                        )
    lines = factor * lines.reshape(planes * breadth, wide * breadth)
    across = np.zeros((depth, depth))
    for k in steps:
        across += second[k] * (np.eye(depth, k=k) + np.eye(depth, k=-k))
    rim = RADIUS * breadth
    inner = lines[:, rim:-rim]
    low = lines[:rim, :rim]
    high = lines[-rim:, -rim:]
    return inner, low, high, factor * across, factor * 3.0 * second[0]


def halves(matrix):
    high = matrix.astype(ml_dtypes.bfloat16)
    low = (matrix - high.astype(np.float64)).astype(ml_dtypes.bfloat16)
    return high, low


def dot(a, b):
    return jnp.dot(a, b, preferred_element_type=F32)


def kernel(
    dims,
    v_hbm,
    pot_hbm,
    proj_hbm,
    inner_h_hbm,
    inner_l_hbm,
    rim_hbm,
    across_hbm,
    gain_ref,
    owner_ref,
    rows_ref,
    wrap_ref,
    out_ref,
    v_ref,
    pot_ref,
    inner_h_ref,
    inner_l_ref,
    rim_ref,
    across_ref,
    sendbuf,
    sendbuf_last,
    relay,
    relay_last,
    arrived,
    arrived_last,
    parts,
    hi_ref,
    halo,
    pick_ref,
    place_ref,
    rim_turned,
    base_ref,
    load_sem,
    piece_sem,
    hop_send,
    hop_recv,
    part_send,
    part_recv,
    share_send,
    share_recv,
    halo_send,
    halo_recv,
):
    n_grid, n_states, tiles, chunk, breadth, nproj, atoms, centre_weight = dims
    cells, depth = v_ref.shape
    breadth_bits, proj_bits = breadth.bit_length() - 1, nproj.bit_length() - 1
    rim = RADIUS * breadth
    count = min(MOST_PIECES, chunk // depth)
    piece = chunk // count
    blocks = piece // depth
    slot_rows = PAIR_CAP * nproj
    me_g, me_s = lax.axis_index("grid"), lax.axis_index("states")
    up, down = lax.rem(me_g + 1, n_grid), lax.rem(me_g + n_grid - 1, n_grid)
    core = lax.rem(me_s, 2)
    side_x, sides = me_s // 2, n_states // 2
    source_s = 2 * side_x + lax.rem(me_g // tiles, 2)
    others = [lax.rem(side_x + d, sides) for d in range(1, sides)]
    partner = me_s + 1 - 2 * lax.rem(me_s, 2)
    twins = [lax.rem(me_s + 2 * d, n_states) for d in range(1, n_states // 2)]

    def start_copy(copy):
        copy.start()

    def await_sent(copy):
        copy.wait_send()

    def outgoing(h, x):
        return sendbuf_last.at[x] if h == count - 1 else sendbuf.at[h, x]

    def relayed(h, x):
        return relay_last.at[x] if h == count - 1 else relay.at[h, x]

    def incoming(h, o):
        return arrived_last.at[o] if h == count - 1 else arrived.at[h, o]

    piece_loads = [
        pltpu.make_async_copy(
            proj_hbm.at[pl.ds(i * slot_rows, slot_rows), pl.ds(s * chunk + h * piece, piece)],
            outgoing(h, s // 2).at[i, s % 2, :, pl.ds(0, piece)],
            piece_sem.at[h, i, s],
        )
        for h in range(count)
        for i in range(tiles)
        for s in range(n_states)
    ]
    load_v, load_pot, *load_tables = [
        pltpu.make_async_copy(src, dst, load_sem.at[n])
        for n, (src, dst) in enumerate(
            (
                (v_hbm, v_ref),
                (pot_hbm, pot_ref),
                (inner_h_hbm, inner_h_ref),
                (inner_l_hbm, inner_l_ref),
                (rim_hbm, rim_ref),
                (across_hbm, across_ref),
            )
        )
    ]
    for load in piece_loads:
        load.start()
    load_v.start()
    load_pot.start()
    for load in load_tables:
        load.start()

    barrier = pltpu.get_barrier_semaphore()

    def greet(g, s):
        pl.semaphore_signal(barrier, inc=1, device_id=(g, s), device_id_type=MESH)

    for o in range(n_grid):

        @pl.when((me_g != o) | (source_s != me_s))
        def _():
            greet(o, source_s)

    greet(up, me_s)
    greet(down, me_s)
    greet(me_g, partner)
    for s in twins:
        greet(me_g, s)

    gain_rows = gain_ref[...]
    nothing = jnp.zeros((slot_rows, depth - nproj), BF16)
    below = jnp.zeros((slot_rows - PAIR_CAP, nproj), BF16)
    for i in range(tiles):
        own_rows = gain_rows[i * PAIR_CAP : (i + 1) * PAIR_CAP]
        block = jnp.concatenate([jnp.concatenate([own_rows, below], axis=0), nothing], axis=1)
        for s in range(n_states):
            sendbuf_last[s // 2, i, s % 2, :, piece:] = block

    pl.semaphore_wait(barrier, n_grid + 2 + len(twins) + jnp.where(source_s == me_s, 0, 1))

    def hop_copy(h, d):
        return pltpu.make_async_remote_copy(
            src_ref=outgoing(h, others[d]),
            dst_ref=relayed(h, side_x),
            send_sem=hop_send.at[h, d],
            recv_sem=hop_recv.at[h, side_x],
            device_id=(me_g, 2 * others[d] + core),
            device_id_type=MESH,
        )

    def await_hop(h, d):
        pltpu.make_async_remote_copy(
            src_ref=outgoing(h, others[d]),
            dst_ref=relayed(h, others[d]),
            send_sem=hop_send.at[h, d],
            recv_sem=hop_recv.at[h, others[d]],
            device_id=(me_g, 2 * others[d] + core),
            device_id_type=MESH,
        ).wait_recv()

    def part_copies(h, d, act):
        x = others[d - 1] if d else side_x
        held = relayed(h, x) if d else outgoing(h, x)
        for i in range(tiles):
            tile = (2 * x + core) * tiles + i
            for c in (1, 0):
                copy = pltpu.make_async_remote_copy(
                    src_ref=held.at[i, c],
                    dst_ref=incoming(h, me_g),
                    send_sem=part_send.at[h, d, i, c],
                    recv_sem=part_recv.at[h, me_g],
                    device_id=(tile, 2 * side_x + c),
                    device_id_type=MESH,
                )
                here = (tile == me_g) & (core == c)

                @pl.when(jnp.logical_not(here))
                def _():
                    act(copy)

                if act is start_copy:

                    @pl.when(here)
                    def _():
                        incoming(h, me_g)[...] = held[i, c]

    def halo_copies(step):
        return [
            pltpu.make_async_remote_copy(
                src_ref=hi_ref.at[step, pl.ds(start, rim)],
                dst_ref=halo.at[step, side],
                send_sem=halo_send.at[step, side],
                recv_sem=halo_recv.at[step, side],
                device_id=(target, me_s),
                device_id_type=MESH,
            )
            for side, start, target in ((0, cells - rim, up), (1, 0, down))
        ]

    def share_copy(h, index, part, target):
        return pltpu.make_async_remote_copy(
            src_ref=parts.at[part, h],
            dst_ref=parts.at[part, h],
            send_sem=share_send.at[h, index],
            recv_sem=share_recv.at[h, part],
            device_id=(me_g, target),
            device_id_type=MESH,
        )

    per_piece = tiles * n_states
    for h in range(count):
        for load in piece_loads[h * per_piece : (h + 1) * per_piece]:
            load.wait()
        for d in range(sides - 1):
            hop_copy(h, d).start()
        if h < 2:
            part_copies(h, 0, start_copy)

    def forward_parts(h):
        for d in range(sides - 1):
            await_hop(h, d)
            part_copies(h, d + 1, start_copy)
        if h + 2 < count:
            part_copies(h + 2, 0, start_copy)

    load_v.wait()
    hi_ref[0] = v_ref[...].astype(BF16)

    owners = [owner_ref[a] for a in range(atoms)]
    slots, ranks = [], []
    for a in range(atoms):
        rank = jnp.int32(0)
        for b in range(a):
            rank = rank + jnp.where(owners[b] == owners[a], 1, 0)
        slots.append(owners[a] * PAIR_CAP + rank)
        ranks.append(rank)
    width = n_grid * slot_rows
    lane = lax.broadcasted_iota(jnp.int32, (nproj, width), 1)
    row = lax.broadcasted_iota(jnp.int32, (nproj, width), 0)
    chosen = jnp.concatenate(
        [jnp.where(lane == slots[a] * nproj + row, 1.0, 0.0) for a in range(atoms)], axis=0
    ).astype(BF16)

    lane = lax.broadcasted_iota(jnp.int32, (1, width), 1)
    places = [owner * slot_rows + rank for owner, rank in zip(owners, ranks)]
    slot_lines = [jnp.where(lane == place, 1.0, 0.0) for place in places]
    slot_lines = jnp.concatenate(
        slot_lines + [jnp.zeros((ATOM_PAD - atoms, width), F32)], axis=0
    ).astype(BF16)
    spread = jnp.where(
        (lax.broadcasted_iota(jnp.int32, (depth, atoms * nproj), 1) & (nproj - 1))
        == lax.broadcasted_iota(jnp.int32, (depth, atoms * nproj), 0),
        1.0,
        0.0,
    ).astype(BF16)

    forward_parts(0)
    block_rows = rows_ref.shape[1]
    local = rows_ref[...] - me_g * cells
    local = jnp.concatenate(
        [local, jnp.full((ATOM_PAD - atoms, block_rows), -1, jnp.int32)], axis=0
    )
    line = lax.broadcasted_iota(jnp.int32, (ATOM_PAD, cells), 1)
    pick = jnp.concatenate(
        [jnp.where(local[:, b : b + 1] == line, 1.0, 0.0) for b in range(block_rows)], axis=0
    )
    pick_ref[...] = pick.astype(BF16)


    def own_cells(step, field):
        hi = hi_ref[step]
        lo = (field - hi.astype(F32)).astype(BF16)
        both = jnp.concatenate([hi, lo], axis=1)
        wide = dot(inner_h_ref[...], both)
        total = base_ref[...] * field
        total = total + (wide[:, :depth] + wide[:, depth:] + dot(inner_l_ref[...], hi))
        across = dot(both, across_ref[...])
        return total + (across[:, :depth] + across[:, depth:])

    def rims(step):
        for copy in halo_copies(step):
            copy.wait_recv()
        sums = []
        for side in range(2):
            came = halo[step, side]
            sums.append(dot(rim_turned[side, 0], came) + dot(rim_turned[side, 1], came))
        middle = jnp.zeros((cells - 2 * rim, depth), F32)
        return jnp.concatenate([sums[0], middle, sums[1]], axis=0)

    def nonlocal_part(step, gains):
        picked = dot(pick_ref[...], hi_ref[step]).astype(BF16)
        coefficients = jnp.zeros((atoms * nproj, ATOM_PAD), F32)
        pairs = [(q, h) for q in range(n_states) for h in range(count)]
        for n, (q, h) in enumerate(pairs):
            lines = [
                picked[b * ATOM_PAD : (b + 1) * ATOM_PAD]
                for b in range(n * blocks, (n + 1) * blocks)
            ]
            coefficients = coefficients + lax.dot_general(
                parts[q, h],
                jnp.concatenate(lines, axis=1),
                (((1,), (1,)), ((), ())),
                preferred_element_type=F32,
            )
        coefficients = coefficients.T
        atom = lax.broadcasted_iota(jnp.int32, coefficients.shape, 0)
        column = lax.broadcasted_iota(jnp.int32, coefficients.shape, 1)
        scaled = jnp.where((column >> proj_bits) == atom, coefficients * gains, 0.0).astype(BF16)
        pieces = []
        for q, h in pairs:
            projected = dot(scaled, parts[q, h]).astype(BF16)
            pieces += [projected[:, b * depth : (b + 1) * depth] for b in range(blocks)]
        return dot(place_ref[...], jnp.concatenate(pieces, axis=0)) * (1.0 / HALF_WIDTH)

    def forward(h):
        for index, s in enumerate(twins):
            share_copy(h, 0, s, partner).wait_recv()
            share_copy(h, 1 + len(twins) + index, s, partner).start()

    def take_share(h):
        for o in range(n_grid):

            @pl.when((me_g != o) | (source_s != me_s))
            def _():
                pltpu.make_async_remote_copy(
                    src_ref=outgoing(h, 0).at[0, 0],
                    dst_ref=incoming(h, o),
                    send_sem=part_send.at[h, 0, 0, 0],
                    recv_sem=part_recv.at[h, o],
                    device_id=(o, source_s),
                    device_id_type=MESH,
                ).wait_recv()

        last = h == count - 1
        came = arrived_last[:, :, :piece] if last else arrived[h]
        parts[me_s, h] = dot(chosen, came.reshape(width, piece)).astype(BF16)
        for index, s in enumerate(twins):
            share_copy(h, 1 + index, me_s, s).start()
        share_copy(h, 0, me_s, partner).start()

    for h in range(1, count):
        forward_parts(h)
        if h >= 2:
            take_share(h - 2)
    for copy in halo_copies(0):
        copy.start()
    place_ref[...] = pick.T.astype(BF16)
    for h in range(max(count - 2, 0), count):
        take_share(h)
    load_pot.wait()
    for load in load_tables:
        load.wait()

    turn = wrap_ref[0]
    source = lax.broadcasted_iota(jnp.int32, (rim, rim), 0)
    target = lax.broadcasted_iota(jnp.int32, (rim, rim), 1)
    low_turn = jnp.where(me_g == 0, turn, 0)
    high_turn = jnp.where(me_g == n_grid - 1, breadth - turn, 0)
    for side, shift in ((0, low_turn), (1, high_turn)):
        same_plane = (source >> breadth_bits) == (target >> breadth_bits)
        moved = ((source + shift) & (breadth - 1)) == (target & (breadth - 1))
        permute = jnp.where(same_plane & moved, 1.0, 0.0).astype(BF16)
        for half in range(2):
            rim_turned[side, half] = dot(rim_ref[side, half], permute).astype(BF16)

    base_ref[...] = (pot_ref[...] - CENTER) * (1.0 / HALF_WIDTH) + centre_weight

    for h in range(count - 1):
        forward(h)
    start = v_ref[...]
    first = own_cells(0, start)
    forward(count - 1)
    first = first + rims(0)
    gain_lines = arrived_last[:, :, piece:].reshape(width, depth)
    gains = dot(dot(slot_lines, gain_lines).astype(BF16), spread)
    for h in range(count):
        share_copy(h, 0, partner, partner).wait_recv()
        for s in twins:
            share_copy(h, 0, s + 1 - 2 * lax.rem(s, 2), partner).wait_recv()

    first = first + nonlocal_part(0, gains)
    hi_ref[1] = first.astype(BF16)
    for copy in halo_copies(1):
        copy.start()
    second = own_cells(1, first) + nonlocal_part(1, gains)
    second = 2.0 * (second + rims(1)) - start
    hi_ref[2] = second.astype(BF16)
    for copy in halo_copies(2):
        copy.start()
    last = own_cells(2, second) + nonlocal_part(2, gains)
    out_ref[...] = (last + rims(2)) - 0.5 * first

    for h in range(count):
        for d in range(sides - 1):
            hop_copy(h, d).wait_send()
        for d in range(sides):
            part_copies(h, d, await_sent)
        share_copy(h, 0, me_s, partner).wait_send()
        for index, s in enumerate(twins):
            share_copy(h, 1 + index, me_s, s).wait_send()
            share_copy(h, 1 + len(twins) + index, s, partner).wait_send()
    for step in range(3):
        for copy in halo_copies(step):
            copy.wait_send()


def shards(states_in, potential, projectors, proj_gains, atom_owner, atom_rows, wrap_rows):
    _, planes, breadth, depth = states_in.shape
    n_grid, n_states = lax.axis_size("grid"), lax.axis_size("states")
    _, held, nproj, span = projectors.shape
    atoms = atom_owner.shape[0]
    cells, rim = planes * breadth, RADIUS * breadth
    tiles = held // PAIR_CAP
    chunk = span // n_states
    count = min(MOST_PIECES, chunk // depth)
    piece, sides = chunk // count, n_states // 2
    slot_rows = PAIR_CAP * nproj
    inner, low, high, across, centre_weight = stencil_matrices(planes, breadth, depth)
    inner_h, inner_l = halves(inner)
    rim_matrices = np.stack([np.stack(halves(low)), np.stack(halves(high))])
    across_h, across_l = halves(across)
    across_both = np.block([[across_h, across_l], [across_h, np.zeros_like(across_l)]])
    dims = (n_grid, n_states, tiles, chunk, breadth, nproj, atoms, centre_weight)
    hbm = pl.BlockSpec(memory_space=pltpu.HBM)
    vmem = pl.BlockSpec(memory_space=pltpu.VMEM)
    smem = pl.BlockSpec(memory_space=pltpu.SMEM)
    flops = 2 * 3 * depth * cells * (5 * cells + 3 * depth)
    out = pl.pallas_call(
        functools.partial(kernel, dims),
        out_shape=jax.ShapeDtypeStruct((cells, depth), F32),
        in_specs=[hbm] * 7 + [vmem, smem, vmem, smem],
        out_specs=vmem,
        scratch_shapes=[
            pltpu.VMEM((cells, depth), F32),
            pltpu.VMEM((cells, depth), F32),
            pltpu.VMEM((cells, cells), BF16),
            pltpu.VMEM((cells, cells), BF16),
            pltpu.VMEM((2, 2, rim, rim), BF16),
            pltpu.VMEM((2 * depth, 2 * depth), BF16),
            pltpu.VMEM((count - 1, sides, tiles, 2, slot_rows, piece), BF16),
            pltpu.VMEM((sides, tiles, 2, slot_rows, piece + depth), BF16),
            pltpu.VMEM((count - 1, sides, tiles, 2, slot_rows, piece), BF16),
            pltpu.VMEM((sides, tiles, 2, slot_rows, piece + depth), BF16),
            pltpu.VMEM((count - 1, n_grid, slot_rows, piece), BF16),
            pltpu.VMEM((n_grid, slot_rows, piece + depth), BF16),
            pltpu.VMEM((n_states, count, atoms * nproj, piece), BF16),
            pltpu.VMEM((3, cells, depth), BF16),
            pltpu.VMEM((3, 2, rim, depth), BF16),
            pltpu.VMEM((ATOM_PAD * atom_rows.shape[1], cells), BF16),
            pltpu.VMEM((cells, ATOM_PAD * atom_rows.shape[1]), BF16),
            pltpu.VMEM((2, 2, rim, rim), BF16),
            pltpu.VMEM((cells, depth), F32),
            pltpu.SemaphoreType.DMA((6,)),
            pltpu.SemaphoreType.DMA((count, tiles, n_states)),
            pltpu.SemaphoreType.DMA((count, sides)),
            pltpu.SemaphoreType.DMA((count, sides)),
            pltpu.SemaphoreType.DMA((count, sides, tiles, 2)),
            pltpu.SemaphoreType.DMA((count, n_grid)),
            pltpu.SemaphoreType.DMA((count, n_states)),
            pltpu.SemaphoreType.DMA((count, n_states)),
            pltpu.SemaphoreType.DMA((3, 2)),
            pltpu.SemaphoreType.DMA((3, 2)),
        ],
        compiler_params=pltpu.CompilerParams(
            collective_id=0, has_side_effects=True, vmem_limit_bytes=63 * 1024 * 1024
        ),
        cost_estimate=pl.CostEstimate(
            flops=flops, bytes_accessed=4 * 1024 * 1024, transcendentals=0
        ),
    )(
        states_in.reshape(cells, depth),
        potential.reshape(cells, depth),
        projectors.reshape(held * nproj, span),
        jnp.asarray(inner_h),
        jnp.asarray(inner_l),
        jnp.asarray(rim_matrices),
        jnp.asarray(across_both),
        proj_gains.reshape(held, nproj),
        atom_owner,
        atom_rows,
        wrap_rows,
    )
    return 2.0 * out.reshape(states_in.shape)


def solution(mesh):
    in_specs = (
        P("states", "grid", None, None),
        P("grid", None, None),
        P("grid", "states", None, None),
        P("grid", "states", None),
        P("grid"),
        P("grid", None),
        P(),
    )
    out_specs = P("states", "grid", None, None)
    return jax.shard_map(shards, mesh=mesh, in_specs=in_specs, out_specs=out_specs, check_vma=False)
```
